256 devices in a mesh: row: 32 (over x, z), col: 8 (over y, core).
Axes of the slice: x: 4, y: 4, z: 8, core: 2. Of those that a mesh axis runs over, the one named last changes fastest.
Arguments:
- site_coords: int32 [3, 8192], P(None, ('row', 'col')), may hold values from 0 to 39
- basis_rows: float32 [8192, 512], P('row'), may hold values from -0.25 to 0.25
- extra_cov: float32 [8192, 8192], P('row', 'col'), may hold values from -2 to 2, as said below
Outputs:
- factored: float32 [8192, 8192], P('row', 'col')
The draws below stay inside these ranges and needn't reach their ends.
Inputs may be any that keep to these rules, and one draw needn't show every extreme that they name: extra_cov[s, t] depends only on the global indices gr(s) and gc(t), is symmetric in them, and the matrix it defines over global sites is positive semidefinite.
All inputs are finite; a program needn't handle non-finite values.
Results may differ from the reference program's by a relative error of at most 0.0003.
Values sent between devices are 32-bit elements; how exact they have to be, the bound alone decides.
No kernel may reach another device: no remote copies, remote signals or barrier semaphores. Data moves between devices by JAX's collectives and lax.ppermute only.
A program may use at most 64 MiB of HBM per device.

```python
import jax
import jax.numpy as jnp
from jax import lax

TILE = 128
GRID_SIDE = 40
BASIS = 512
EXTRA = 512
PANEL = 512
N = 8192
N_ROW = 32
N_COL = 8


def global_of_stored(count, groups, tile):
    positions = jnp.arange(count, dtype=jnp.int32)
    share = count // groups
    owner_group = positions // share
    within_tile = positions % share
    return (within_tile // tile * groups + owner_group) * tile + within_tile % tile


def draw_extra_cov(key, part):
    key = jax.random.fold_in(key, 7)
    factors = jax.random.randint(key, (N, EXTRA), -2, 3).astype(jnp.float32)
    row_global = global_of_stored(N, N_ROW, TILE)
    col_global = global_of_stored(N, N_COL, TILE)
    row_factors = factors[row_global]
    col_factors = factors[col_global]
    product = jnp.dot(row_factors, col_factors.T, precision=lax.Precision.HIGHEST, preferred_element_type=jnp.float32)
    return product * (0.5 / EXTRA)


def place_ends(entries, own_key, smallest, high):
    dims = entries.shape
    spot = [jax.random.randint(jax.random.fold_in(own_key, axis), (), 0, dims[axis]) for axis in range(len(dims))]
    entries = entries.at[tuple(spot)].set(smallest)
    longest = dims.index(max(dims))
    spot[longest] = (spot[longest] + 1) % dims[longest]
    return entries.at[tuple(spot)].set(high)


def steps_of(key, dims, pieces, least, top_value):
    loudness, own = 1.0, jax.random.fold_in(key, 6)
    for position, blocks in pieces:
        steps = jnp.exp(jax.random.uniform(jax.random.fold_in(own, position), (blocks,), jnp.float32, least / len(pieces), top_value / len(pieces)))
        loudness = loudness * jnp.repeat(steps, dims[position] // blocks).reshape([-1 if axis == position else 1 for axis in range(len(dims))])
    return loudness


def centred(key, extent, scale, most, split=(), kind=jnp.bfloat16):
    drawn = scale * jax.random.normal(key, extent, jnp.float32)
    if split:
        drawn = drawn * steps_of(key, extent, split, -0.22, 0.18)
    return jnp.clip(drawn, -most, most).astype(kind)


def setup_inputs(seed: int = 0) -> dict:
    key_of = jax.random.split(jax.random.key(seed), 4)
    return {
        "site_coords": place_ends(jax.random.randint(key_of[0], (3, N), 0, GRID_SIDE), jax.random.fold_in(key_of[0], 1), 0, GRID_SIDE - 1).astype(jnp.int32),
        "basis_rows": centred(key_of[1], (N, BASIS), BASIS ** -0.5, 0.25, ((0, 32),), jnp.float32),
        "extra_cov": draw_extra_cov(jax.random.fold_in(key_of[3], 71), 0),
    }


nugget = 0.5
range_cells = 3.0

def covariance(first_sites, second_sites, first_global, second_global, first_basis, second_basis):
    first_sq = lax.optimization_barrier(jnp.sum(first_sites * first_sites, axis=0))
    second_sq = lax.optimization_barrier(jnp.sum(second_sites * second_sites, axis=0))
    inner_prod = jnp.dot(first_sites.T.astype(jnp.float32), second_sites.astype(jnp.float32), precision=lax.Precision.HIGHEST, preferred_element_type=jnp.float32)
    squared = first_sq[:, None] + second_sq[None, :] - 2.0 * inner_prod
    kernel = jnp.exp(-jnp.sqrt(squared) / range_cells)
    basis_term = jnp.dot(first_basis.astype(jnp.float32), second_basis.T.astype(jnp.float32), precision=lax.Precision.HIGHEST, preferred_element_type=jnp.float32)
    return kernel + jnp.where(first_global[:, None] == second_global[None, :], nugget, 0.0) + basis_term

def stored_global(count, groups, tile):
    positions = jnp.arange(count, dtype=jnp.int32)
    share = count // groups
    owner_group = positions // share
    within_tile = positions % share
    return (within_tile // tile * groups + owner_group) * tile + within_tile % tile

def stored_place(count, groups, tile):
    positions = jnp.arange(count, dtype=jnp.int32)
    tile_number = positions // tile
    return tile_number % groups * (count // groups) + tile_number // groups * tile + positions % tile

def reference(site_coords, basis_rows, extra_cov):
    site_count = site_coords.shape[1]
    row_global = stored_global(site_count, N_ROW, TILE)
    col_global = stored_global(site_count, N_COL, TILE)
    row_place = stored_place(site_count, N_ROW, TILE)
    col_place = stored_place(site_count, N_COL, TILE)
    site_floats = site_coords.astype(jnp.float32)
    row_sites = site_floats[:, row_global]
    col_sites = site_floats[:, col_global]
    col_basis = basis_rows[row_place[col_global]]
    blocks = site_count // PANEL

    def build_rows(block_items):
        block_sites, block_global, block_basis, block_extra = block_items
        return covariance(block_sites, col_sites, block_global, col_global, block_basis, col_basis) + block_extra
    matrix = lax.map(build_rows, (row_sites.reshape(3, blocks, PANEL).transpose(1, 0, 2), row_global.reshape(blocks, PANEL), basis_rows.reshape(blocks, PANEL, BASIS), extra_cov.reshape(blocks, PANEL, site_count)))
    matrix = matrix.reshape(site_count, site_count)
    lefts = []
    for number in range(2):
        start = number * PANEL
        strip = matrix[:, col_place[start:start + PANEL]]
        diag_block = strip[row_place[start:start + PANEL]]
        lower_chol = jnp.linalg.cholesky(diag_block)
        inverse = lax.linalg.triangular_solve(lower_chol, jnp.eye(PANEL, dtype=jnp.float32), left_side=True, lower=True)
        left_factor = jnp.dot(strip.astype(jnp.float32), inverse.T.astype(jnp.float32), precision=lax.Precision.HIGHEST, preferred_element_type=jnp.float32)
        keep_mask = row_global[:, None] - start >= jnp.arange(PANEL, dtype=jnp.int32)[None, :]
        left_factor = jnp.where(keep_mask, left_factor, 0.0)
        right_factor = left_factor[row_place[col_global]]

        def update(block_items):
            row_block, factor_rows = block_items
            return row_block - jnp.dot(factor_rows.astype(jnp.float32), right_factor.T.astype(jnp.float32), precision=lax.Precision.HIGHEST, preferred_element_type=jnp.float32)
        matrix = lax.map(update, (matrix.reshape(blocks, PANEL, site_count), left_factor.reshape(blocks, PANEL, PANEL)))
        matrix = matrix.reshape(site_count, site_count)
        lefts.append(left_factor)
    matrix = matrix.at[row_place[:2 * PANEL], :].set(0.0)
    matrix = matrix.at[:, col_place[:2 * PANEL]].set(jnp.concatenate(lefts, 1))
    return matrix
```

```python
import functools

import jax
import jax.numpy as jnp
from jax import lax
from jax.experimental import pallas as pl
from jax.experimental.pallas import tpu as pltpu
from jax.sharding import PartitionSpec as P

TILE = 128
PANEL = 512
FIRST = 1024
BLOCK = 32
NX, NZ, NC = 4, 8, 8

nugget = 0.5
range_cells = 3.0
highest = lax.Precision.HIGHEST
BOTH = ("row", "col")


def dot_nn(a, b):
    return lax.dot_general(
        a, b, (((1,), (0,)), ((), ())), precision=highest, preferred_element_type=jnp.float32
    )


def dot_nt(a, b):
    return lax.dot_general(
        a, b, (((1,), (1,)), ((), ())), precision=highest, preferred_element_type=jnp.float32
    )


def dot_tn(a, b):
    return lax.dot_general(
        a, b, (((0,), (0,)), ((), ())), precision=highest, preferred_element_type=jnp.float32
    )


def reciprocal(x):
    r = pl.reciprocal(x, approx=True)
    return r * (2.0 - x * r)


def factor_tile(t):
    row = lax.broadcasted_iota(jnp.int32, (TILE, TILE), 0)
    lane = lax.broadcasted_iota(jnp.int32, (TILE, TILE), 1)
    sub = lax.broadcasted_iota(jnp.int32, (BLOCK, TILE), 0)
    w = jnp.where(row == lane, 1.0, 0.0).astype(jnp.float32)
    uppers, inverses = [], []
    for k in range(0, TILE, BLOCK):
        p, x = t[:BLOCK], w[:BLOCK]
        cols = [jnp.broadcast_to(p[:, k + q : k + q + 1], (BLOCK, TILE)) for q in range(BLOCK)]
        pivots = jnp.zeros((BLOCK, TILE), jnp.float32)
        for q in range(BLOCK):
            pivot = jnp.broadcast_to(cols[q][q : q + 1], (BLOCK, TILE))
            pivots = jnp.where(sub == q, pivot, pivots)
            if q < BLOCK - 1:
                m = jnp.where(sub > q, cols[q], 0.0) * reciprocal(pivot)
                for s in range(q + 1, BLOCK):
                    cols[s] = cols[s] - m * jnp.broadcast_to(cols[s][q : q + 1], (BLOCK, TILE))
                p = p - m * jnp.broadcast_to(p[q : q + 1], (BLOCK, TILE))
                x = x - m * jnp.broadcast_to(x[q : q + 1], (BLOCK, TILE))
        scale = lax.rsqrt(pivots)
        p, x = p * scale, x * scale
        uppers.append(p)
        inverses.append(x)
        if k + BLOCK < TILE:
            prod = dot_tn(p, jnp.concatenate([p, x], axis=1))[k + BLOCK :]
            t = t[BLOCK:] - prod[:, :TILE]
            w = w[BLOCK:] - prod[:, TILE:]
    u = jnp.where(lane >= row, jnp.concatenate(uppers, 0), 0.0)
    return u, jnp.concatenate(inverses, 0)


def inverse_kernel(tiles, a_ref, v_ref, work):
    n = tiles * TILE
    work[:, :n] = a_ref[...]
    work[:, n:] = jnp.zeros((n, n), jnp.float32)

    def step(j, carry):
        first = pl.multiple_of(j * TILE, TILE)
        rows = pl.ds(first, TILE)
        u, v = factor_tile(work[rows, rows])
        work[rows, :] = dot_nn(v, work[rows, :])
        work[rows, rows] = u
        work[rows, pl.ds(pl.multiple_of(n + first, TILE), TILE)] = v

        def update(i, inner):
            below = pl.ds(pl.multiple_of(i * TILE, TILE), TILE)
            work[below, :] = work[below, :] - dot_tn(work[rows, below], work[rows, :])
            return inner

        lax.fori_loop(j + 1, tiles, update, 0)
        return carry

    lax.fori_loop(0, tiles, step, 0)
    v_ref[...] = work[:, n:]


def cholesky_inverse(a):
    n = a.shape[0]
    return pl.pallas_call(
        functools.partial(inverse_kernel, n // TILE),
        out_shape=jax.ShapeDtypeStruct((n, n), jnp.float32),
        in_specs=[pl.BlockSpec(memory_space=pltpu.VMEM)],
        out_specs=pl.BlockSpec(memory_space=pltpu.VMEM),
        scratch_shapes=[pltpu.VMEM((n, 2 * n), jnp.float32)],
        compiler_params=pltpu.CompilerParams(vmem_limit_bytes=40 * 2**20),
        cost_estimate=pl.CostEstimate(flops=10**9, bytes_accessed=10**8, transcendentals=0),
    )(a)


def kernel_of(a, b):
    squared = sum((a[d][:, None] - b[d][None, :]) ** 2 for d in range(3))
    return jnp.exp(-jnp.sqrt(squared) / range_cells)


def spread_to(value, axis, count, groups=None):
    every = jnp.broadcast_to(value[None], (count,) + value.shape)
    return lax.all_to_all(every, axis, 0, 0, axis_index_groups=groups)


def from_first_x(value, swap):
    parts = []
    for x in range(NX):
        if x == 0 and not swap:
            continue
        pairs = [
            (z * NC + c, (x * NZ + z) * NC + ((c + 4) % NC if swap else c))
            for z in range(NZ)
            for c in range(NC)
        ]
        parts.append(lax.ppermute(value, BOTH, pairs))
    if not swap:
        parts.append(jnp.where(lax.axis_index("row") < NZ, value, 0.0))
    return sum(parts[1:], parts[0])


def around_col(value, my_col):
    parts = [value] + [
        lax.ppermute(value, "col", [(c, (c + k) % NC) for c in range(NC)]) for k in range(1, NC)
    ]
    stacked = jnp.stack(parts[::-1] + parts[::-1])
    return lax.dynamic_slice_in_dim(stacked, NC - 1 - my_col, NC, 0)


def local(site_coords, basis_rows, extra_cov):
    my_row = lax.axis_index("row")
    my_col = lax.axis_index("col")
    z_groups = [[x * NZ + z for z in range(NZ)] for x in range(NX)]
    strip = extra_cov[:, :TILE]

    turn = [
        ((x * NZ + z) * NC + c, (x * NZ + c) * NC + z)
        for x in range(NX)
        for z in range(NZ)
        for c in range(NC)
    ]
    basis_part = lax.dynamic_slice_in_dim(basis_rows, my_col * 32, 32, 0).reshape(128, 128)
    turned = lax.ppermute(jnp.concatenate([strip, basis_part]), BOTH, turn)
    cols_all = lax.all_gather(turned, "row", axis=0)

    low = my_col < 4
    top, bottom = strip[:64], strip[64:TILE]
    basis_16 = lax.dynamic_slice_in_dim(basis_rows, my_col * 16, 16, 0).reshape(64, 128)
    kept = from_first_x(jnp.concatenate([jnp.where(low, top, bottom), basis_16]), False)
    swapped = from_first_x(jnp.where(low, bottom, top), True)
    lo_half = jnp.where(low, kept[:64], swapped)
    hi_half = jnp.where(low, swapped, kept[:64])
    over_z = spread_to(jnp.concatenate([lo_half, kept[64:], hi_half]), "row", NZ, z_groups)
    panel_part = over_z[:4, :128]
    rest_part = jnp.concatenate([over_z[4:].reshape(4 * 192, 128), strip])
    panel_all = spread_to(panel_part, "col", NC)
    rest_all = around_col(rest_part, my_col)

    sites = spread_to(site_coords, BOTH, 256)
    sites = sites.astype(jnp.float32).transpose(1, 0, 2).reshape(3, 8192)
    first_sites = sites[:, :FIRST]
    row_sites = lax.dynamic_index_in_dim(
        sites.reshape(3, 2, 32, TILE), my_row, 2, keepdims=False
    ).reshape(3, 256)
    col_sites = lax.dynamic_index_in_dim(
        sites.reshape(3, 8, 8, TILE), my_col, 2, keepdims=False
    ).reshape(3, 1024)

    def halves(part):
        return part.reshape(2, 4, 4, 64, 128).transpose(2, 0, 3, 1, 4).reshape(512, 512)

    def basis_of(part):
        return part.reshape(8, 4, 16, 512).transpose(1, 0, 2, 3).reshape(512, 512)

    eye = 0.5 * jnp.eye(PANEL, dtype=jnp.float32)
    sites0, sites1 = first_sites[:, :PANEL], first_sites[:, PANEL:]
    extra00 = halves(panel_all[:, :, :64])
    basis0 = basis_of(panel_all[:, :, 64:])
    a00 = extra00 + kernel_of(sites0, sites0) + eye + dot_nt(basis0, basis0)
    v00 = cholesky_inverse(a00)

    rest_z = rest_all[:, : 4 * 192].reshape(8, 4, 192, 128)
    extra10 = halves(rest_z[:, :, :64])
    basis1 = basis_of(rest_z[:, :, 64:128])
    extra11 = halves(rest_z[:, :, 128:])
    a10 = extra10 + kernel_of(sites1, sites0) + dot_nt(basis1, basis0)
    a11 = extra11 + kernel_of(sites1, sites1) + eye + dot_nt(basis1, basis1)
    l10 = dot_nt(a10, v00)
    v11 = cholesky_inverse(a11 - dot_nt(l10, l10))

    positions = jnp.arange(256, dtype=jnp.int32)
    row_global = (positions // TILE * 32 + my_row) * TILE + positions % TILE
    panel_index = jnp.arange(PANEL, dtype=jnp.int32)
    extra_r = rest_all[:, 4 * 192 :].transpose(1, 0, 2).reshape(256, FIRST)
    basis_first = jnp.concatenate([basis0, basis1])
    same = row_global[:, None] == jnp.arange(FIRST, dtype=jnp.int32)[None, :]
    a_r = (
        extra_r
        + kernel_of(row_sites, first_sites)
        + jnp.where(same, nugget, 0.0)
        + dot_nt(basis_rows, basis_first)
    )
    left0 = dot_nt(a_r[:, :PANEL], v00)
    left0 = jnp.where(row_global[:, None] >= panel_index[None, :], left0, 0.0)
    left1 = dot_nt(a_r[:, PANEL:] - dot_nt(left0, l10), v11)
    left1 = jnp.where(row_global[:, None] - PANEL >= panel_index[None, :], left1, 0.0)
    m1 = dot_nn(left1, v11)
    m0 = dot_nn(left0 - dot_nn(m1, l10), v00)
    m = jnp.concatenate([m0, m1], axis=1)

    shaped = cols_all.reshape(NX, NZ, 384, 128)
    extra_c = shaped[:, :, :256].reshape(4, 8, 2, 128, 128).transpose(2, 0, 3, 1, 4)
    extra_c = extra_c.reshape(1024, FIRST)[TILE:]
    basis_c = shaped[:, :, 256:].reshape(4, 2, 128, 512).transpose(1, 0, 2, 3)
    basis_c = basis_c.reshape(1024, 512)[TILE:]
    rest_sites = col_sites[:, TILE:]
    rest_position = jnp.arange(TILE, 1024, dtype=jnp.int32)
    rest_global = (rest_position // TILE * 8 + my_col) * TILE + rest_position % TILE
    cross = extra_c + kernel_of(rest_sites, first_sites)
    basis_m = basis_rows - dot_nn(m, basis_first)
    trailing = (
        extra_cov[:, TILE:]
        + kernel_of(row_sites, rest_sites)
        + jnp.where(row_global[:, None] == rest_global[None, :], nugget, 0.0)
        + dot_nt(basis_m, basis_c)
        - dot_nt(m, cross)
    )
    trailing = jnp.where(row_global[:, None] < FIRST, 0.0, trailing)
    lefts = jnp.concatenate([left0, left1], axis=1)
    own = lax.dynamic_slice_in_dim(lefts, my_col * TILE, TILE, 1)
    return jnp.concatenate([own, trailing], axis=1)


def solution(mesh):
    in_specs = (P(None, BOTH), P("row", None), P("row", "col"))
    out_specs = P("row", "col")
    return jax.shard_map(local, mesh=mesh, in_specs=in_specs, out_specs=out_specs, check_vma=False)
```

```python
import jax
import jax.numpy as jnp
from jax import lax
from jax.experimental import pallas as pl
from jax.experimental.pallas import tpu as pltpu
from jax.sharding import PartitionSpec as P

TILE = 128
PANEL = 512
FIRST = 1024
BLOCK = 32
NX, NZ, NC = 4, 8, 8

nugget = 0.5
range_cells = 3.0
highest = lax.Precision.HIGHEST
BOTH = ("row", "col")


def dot_nn(a, b):
    return lax.dot_general(
        a, b, (((1,), (0,)), ((), ())), precision=highest, preferred_element_type=jnp.float32
    )


def dot_nt(a, b):
    return lax.dot_general(
        a, b, (((1,), (1,)), ((), ())), precision=highest, preferred_element_type=jnp.float32
    )


def dot_tn(a, b):
    return lax.dot_general(
        a, b, (((0,), (0,)), ((), ())), precision=highest, preferred_element_type=jnp.float32
    )


def times_lower_t(a, v):
    half = v.shape[0] // 2
    return jnp.concatenate([dot_nt(a[:, :half], v[:half, :half]), dot_nt(a, v[half:, :])], axis=1)


def times_lower(a, v):
    half = v.shape[0] // 2
    return jnp.concatenate([dot_nn(a, v[:, :half]), dot_nn(a[:, half:], v[half:, half:])], axis=1)


def near_dot(a, b):
    return jnp.exp(jnp.sqrt(jnp.maximum(dot_tn(a, b), 0.0)) * (-1.0 / range_cells))


def reciprocal(x):
    r = pl.reciprocal(x, approx=True)
    return r * (2.0 - x * r)


def factor_tile(t):
    row = lax.broadcasted_iota(jnp.int32, (TILE, TILE), 0)
    lane = lax.broadcasted_iota(jnp.int32, (TILE, TILE), 1)
    sub = lax.broadcasted_iota(jnp.int32, (BLOCK, TILE), 0)
    w = jnp.where(row == lane, 1.0, 0.0).astype(jnp.float32)
    uppers, inverses = [], []
    for k in range(0, TILE, BLOCK):
        p, x = t[:BLOCK], w[:BLOCK]
        cols = [jnp.broadcast_to(p[:, k + q : k + q + 1], (BLOCK, TILE)) for q in range(BLOCK)]
        pivots = jnp.zeros((BLOCK, TILE), jnp.float32)
        for q in range(BLOCK):
            pivot = jnp.broadcast_to(cols[q][q : q + 1], (BLOCK, TILE))
            pivots = jnp.where(sub == q, pivot, pivots)
            if q < BLOCK - 1:
                m = jnp.where(sub > q, cols[q], 0.0) * reciprocal(pivot)
                for s in range(q + 1, BLOCK):
                    cols[s] = cols[s] - m * jnp.broadcast_to(cols[s][q : q + 1], (BLOCK, TILE))
                p = p - m * jnp.broadcast_to(p[q : q + 1], (BLOCK, TILE))
                x = x - m * jnp.broadcast_to(x[q : q + 1], (BLOCK, TILE))
        scale = lax.rsqrt(pivots)
        p, x = p * scale, x * scale
        uppers.append(p)
        inverses.append(x)
        if k + BLOCK < TILE:
            prod = dot_tn(p, jnp.concatenate([p, x], axis=1))[k + BLOCK :]
            t = t[BLOCK:] - prod[:, :TILE]
            w = w[BLOCK:] - prod[:, TILE:]
    u = jnp.where(lane >= row, jnp.concatenate(uppers, 0), 0.0)
    return u, jnp.concatenate(inverses, 0)


def factor_in_place(work, tiles):
    n = tiles * TILE

    for j in range(tiles):
        rows = slice(j * TILE, (j + 1) * TILE)
        u, v = factor_tile(work[rows, rows])
        live = slice((j + 1) * TILE, n + j * TILE)
        if tiles > 1:
            work[rows, live] = dot_nn(v, work[rows, live])
        work[rows, rows] = u
        work[rows, n + j * TILE : n + (j + 1) * TILE] = v
        below = slice((j + 1) * TILE, n)
        if j + 1 < tiles:
            wide = slice((j + 1) * TILE, n + (j + 1) * TILE)
            work[below, wide] = work[below, wide] - dot_tn(work[rows, below], work[rows, wide])


def place_basis(parts, offset, basis):
    for c in range(NC):
        for z in range(4):
            for l in range(4):
                basis[z * TILE + c * 16 : z * TILE + c * 16 + 16, l * TILE : (l + 1) * TILE] = (
                    parts[c, z, offset + l * 16 : offset + l * 16 + 16, :]
                )


def extra_rows(parts, offset, z):
    halves = []
    for h in range(2):
        halves.append(
            jnp.concatenate(
                [parts[h * 4 + q, z, offset : offset + 64, :] for q in range(4)], axis=1
            )
        )
    return jnp.concatenate(halves, axis=0)


def panel0_kernel(parts, left_feat, right_feat, v_ref, basis, work):
    place_basis(parts, 64, basis)
    work[:, PANEL:] = jnp.zeros((PANEL, PANEL), jnp.float32)
    for z in range(0, 4, 2):
        rows = slice(z * TILE, (z + 2) * TILE)
        extra = jnp.concatenate([extra_rows(parts, 0, z), extra_rows(parts, 0, z + 1)], axis=0)
        near = near_dot(left_feat[:, rows], right_feat[:, :PANEL])
        work[rows, :PANEL] = extra + near + dot_nt(basis[rows, :], basis[...])
    add_nugget(work)
    factor_in_place(work, 4)
    v_ref[...] = work[:, PANEL:]


def add_nugget(work):
    row = lax.broadcasted_iota(jnp.int32, (TILE, TILE), 0)
    lane = lax.broadcasted_iota(jnp.int32, (TILE, TILE), 1)
    diagonal = jnp.where(row == lane, nugget, 0.0).astype(jnp.float32)
    for z in range(4):
        rows = slice(z * TILE, (z + 1) * TILE)
        work[rows, rows] = work[rows, rows] + diagonal


def rows0_kernel(my_row, strips, v0, basis0, basis_rows, near_rows, left0):
    extra = jnp.concatenate([strips[q] for q in range(4)], axis=1)
    a = extra + near_rows[:, :PANEL] + dot_nt(basis_rows[...], basis0[...])
    left0[...] = keep_lower(times_lower_t(a, v0[...]), my_row, 0)


def keep_lower(value, my_row, start):
    lane = lax.broadcasted_iota(jnp.int32, (256, PANEL), 1)
    row = lax.broadcasted_iota(jnp.int32, (256, PANEL), 0)
    row_global = jnp.where(row < TILE, row + my_row[0] * TILE, row + 32 * TILE)
    return jnp.where(row_global - start >= lane, value, 0.0)


def panel1_kernel(
    my_row, parts, strips, v0, basis0, basis_rows, left_feat, right_feat, near_rows, left0,
    left, m, basis_m, work, basis1, l10,
):
    place_basis(parts, 64, basis1)
    work[:, PANEL:] = jnp.zeros((PANEL, PANEL), jnp.float32)
    for z in range(0, 4, 2):
        rows = slice(z * TILE, (z + 2) * TILE)
        feat = left_feat[:, PANEL + z * TILE : PANEL + (z + 2) * TILE]
        near = near_dot(feat, right_feat[...])
        extra = jnp.concatenate([extra_rows(parts, 0, z), extra_rows(parts, 0, z + 1)], axis=0)
        a10 = extra + near[:, :PANEL] + dot_nt(basis1[rows, :], basis0[...])
        l10[rows, :] = times_lower_t(a10, v0[...])
        extra = jnp.concatenate([extra_rows(parts, 128, z), extra_rows(parts, 128, z + 1)], axis=0)
        work[rows, :PANEL] = extra + near[:, PANEL:]
    for z in range(0, 4, 2):
        rows = slice(z * TILE, (z + 2) * TILE)
        cols = slice(z * TILE, PANEL)
        work[rows, cols] = (
            work[rows, cols]
            + dot_nt(basis1[rows, :], basis1[cols, :])
            - dot_nt(l10[rows, :], l10[cols, :])
        )
    add_nugget(work)
    extra = jnp.concatenate([strips[4 + q] for q in range(4)], axis=1)
    left[:, PANEL:] = (
        extra
        + near_rows[:, PANEL:]
        + dot_nt(basis_rows[...], basis1[...])
        - dot_nt(left0[...], l10[...])
    )
    left[:, :PANEL] = left0[...]
    factor_in_place(work, 4)
    v1 = work[:, PANEL:]
    left1 = keep_lower(times_lower_t(left[:, PANEL:], v1), my_row, PANEL)
    left[:, PANEL:] = left1
    m1 = times_lower(left1, v1)
    m[:, PANEL:] = m1
    m0 = times_lower(left0[...] - dot_nn(m1, l10[...]), v0[...])
    m[:, :PANEL] = m0
    basis_m[...] = basis_rows[...] - dot_nn(m0, basis0[...]) - dot_nn(m1, basis1[...])


def trailing_kernel(place, parts, near_low, near_high, base, left, m, basis_m, out):
    x = pl.program_id(0)
    cross = jnp.concatenate([parts[0, c, :256, :] for c in range(NC)], axis=1)
    cross = cross + jnp.concatenate([near_low[...], near_high[...]], axis=0)
    basis_c = jnp.concatenate(
        [
            jnp.concatenate(
                [parts[0, c, 256 + l * 32 : 288 + l * 32, :] for l in range(4)], axis=1
            )
            for c in range(NC)
        ],
        axis=0,
    )
    value = dot_nt(basis_m[...], basis_c) - dot_nt(m[...], cross)
    row = lax.broadcasted_iota(jnp.int32, (256, TILE), 0)
    zero = (row < TILE) & (place[0] < 8)
    for k in range(2):
        cols = pl.ds(pl.multiple_of((k * 4 + x) * TILE, TILE), TILE)
        part = value[:, k * TILE : (k + 1) * TILE] + base[:, cols]
        out[:, cols] = jnp.where(zero, 0.0, part)

    @pl.when(x == 0)
    def _():
        out[:, :TILE] = left[:, pl.ds(pl.multiple_of(place[1] * TILE, TILE), TILE)]


VMEM = pl.BlockSpec(memory_space=pltpu.VMEM)
SMEM = pl.BlockSpec(memory_space=pltpu.SMEM)


def floats(*shape):
    return jax.ShapeDtypeStruct(shape, jnp.float32)


def params():
    return pltpu.CompilerParams(vmem_limit_bytes=48 * 2**20)


def cost(us):
    return pl.CostEstimate(flops=us * 10**9, bytes_accessed=us * 3 * 10**6, transcendentals=0)


def panel0(*args):
    return pl.pallas_call(
        panel0_kernel,
        out_shape=[floats(PANEL, PANEL), floats(PANEL, PANEL)],
        in_specs=[VMEM] * 3,
        out_specs=[VMEM] * 2,
        scratch_shapes=[pltpu.VMEM((PANEL, 2 * PANEL), jnp.float32)],
        compiler_params=params(),
        cost_estimate=cost(30),
    )(*args)


def rows0(*args):
    return pl.pallas_call(
        rows0_kernel,
        out_shape=floats(256, PANEL),
        in_specs=[SMEM] + [VMEM] * 5,
        out_specs=VMEM,
        compiler_params=params(),
        cost_estimate=cost(4),
    )(*args)


def panel1(*args):
    return pl.pallas_call(
        panel1_kernel,
        out_shape=[floats(256, FIRST), floats(256, FIRST), floats(256, PANEL)],
        in_specs=[SMEM] + [VMEM] * 9,
        out_specs=[VMEM] * 3,
        scratch_shapes=[
            pltpu.VMEM((PANEL, 2 * PANEL), jnp.float32),
            pltpu.VMEM((PANEL, PANEL), jnp.float32),
            pltpu.VMEM((PANEL, PANEL), jnp.float32),
        ],
        compiler_params=params(),
        cost_estimate=cost(40),
    )(*args)


def trailing(place, parts, near_cols, base, left, m, basis_m):
    def whole(width):
        return pl.BlockSpec((256, width), lambda x: (0, 0))

    return pl.pallas_call(
        trailing_kernel,
        grid=(4,),
        out_shape=floats(256, FIRST),
        in_specs=[
            SMEM,
            pl.BlockSpec((1, NC, 384, TILE), lambda x: (x, 0, 0, 0)),
            pl.BlockSpec((TILE, FIRST), lambda x: (x, 0)),
            pl.BlockSpec((TILE, FIRST), lambda x: (x + 4, 0)),
            whole(FIRST),
            whole(FIRST),
            whole(FIRST),
            whole(PANEL),
        ],
        out_specs=whole(FIRST),
        compiler_params=params(),
        cost_estimate=cost(8),
    )(place, parts, near_cols, near_cols, base, left, m, basis_m)


def kernel_of(a, b):
    squared = sum((a[d][:, None] - b[d][None, :]) ** 2 for d in range(3))
    return jnp.exp(-jnp.sqrt(squared) / range_cells)


def spread_to(value, axis, count, groups=None):
    every = jnp.broadcast_to(value[None], (count,) + value.shape)
    return lax.all_to_all(every, axis, 0, 0, axis_index_groups=groups)


def after(value, done):
    return jnp.where(done == done, value, jnp.zeros_like(value))


def lane_groups(rows):
    n = rows.shape[0]
    return rows.reshape(n, 4, TILE).transpose(1, 0, 2).reshape(4 * n, TILE)


def local(site_coords, basis_rows, extra_cov):
    my_row = lax.axis_index("row")
    my_col = lax.axis_index("col")
    z_groups = [[x * NZ + z for z in range(NZ)] for x in range(NX)]
    strip = extra_cov[:, :TILE]

    half = my_col // 4
    own_sites = jnp.pad(site_coords.astype(jnp.float32).reshape(1, 96), ((0, 7), (0, 32)))
    packs = []
    for h in range(2):
        piece = (my_col % 4 + 4 * h) * 16
        basis_16 = lane_groups(lax.dynamic_slice_in_dim(basis_rows, piece, 16, 0))
        basis_8 = lax.dynamic_slice_in_dim(basis_16, half * 32, 32, 0)
        packs.append(jnp.concatenate([strip[h * 64 : h * 64 + 64], basis_8, own_sites]))
    x_groups = [
        [(x * NZ + z) * NC + q + 4 * h for x in range(NX) for h in range(2)]
        for z in range(NZ)
        for q in range(4)
    ]
    over_x = lax.all_to_all(jnp.stack(packs * NX), BOTH, 0, 0, axis_index_groups=x_groups)
    first_of = jnp.where(half == 0, over_x[0, 96:], over_x[1, 96:])
    pack = jnp.concatenate(
        [over_x[0, :64], over_x[0, 64:96], over_x[1, 64:96], first_of, over_x[1, :64]]
    )
    over_z = spread_to(pack, "row", NZ, z_groups)
    panel_all = spread_to(over_z[:4, :136], "col", NC)
    rest = jnp.concatenate([over_z[4:, :128], over_z[4:, 136:]], axis=1)
    done = panel_all[0, 0, 0, 0]
    rest_all = spread_to(after(rest, done), "col", NC)

    first_sites = panel_all[:, :, 128, :96].reshape(NC, 4, 3, 32)
    first_sites = first_sites.transpose(2, 1, 0, 3).reshape(3, FIRST)
    square = jnp.sum(first_sites * first_sites, axis=0, keepdims=True)
    one, none = jnp.ones_like(square), jnp.zeros_like(square)
    left_feat = jnp.concatenate([first_sites, square, one, none, none, none])
    right_feat = jnp.concatenate([-2.0 * first_sites, one, square, none, none, none])
    sites = spread_to(after(site_coords, done), BOTH, 256)
    sites = sites.astype(jnp.float32).transpose(1, 0, 2).reshape(3, 8192)
    row_sites = lax.dynamic_index_in_dim(
        sites.reshape(3, 2, 32, TILE), my_row, 2, keepdims=False
    ).reshape(3, 256)
    col_sites = lax.dynamic_index_in_dim(
        sites.reshape(3, 8, 8, TILE), my_col, 2, keepdims=False
    ).reshape(3, 1024)
    first_global = jnp.arange(FIRST, dtype=jnp.int32)
    stored = jnp.arange(1024, dtype=jnp.int32)
    row_global = (stored[:256] // TILE * 32 + my_row) * TILE + stored[:256] % TILE
    col_global = (stored // TILE * 8 + my_col) * TILE + stored % TILE

    def near_of(a, b, a_global, b_global):
        return kernel_of(a, b) + jnp.where(a_global[:, None] == b_global[None, :], nugget, 0.0)

    near_rows = near_of(row_sites, first_sites, row_global, first_global)
    near_cols = kernel_of(col_sites, first_sites)
    base = near_of(row_sites, col_sites, row_global, col_global) + extra_cov

    turn = [
        ((x * NZ + z) * NC + c, (x * NZ + c) * NC + z)
        for x in range(NX)
        for z in range(NZ)
        for c in range(NC)
    ]
    basis_part = lane_groups(lax.dynamic_slice_in_dim(basis_rows, my_col * 32, 32, 0))
    turning = after(jnp.concatenate([strip, basis_part]), over_x[0, 0, 0])
    turned = lax.ppermute(turning, BOTH, turn)
    cols_all = lax.all_gather(turned, "row", axis=0)
    strips = lax.all_gather(strip, "col", axis=0)

    v0, basis0 = panel0(panel_all, left_feat, right_feat)
    row_number = my_row.reshape(1)
    left0 = rows0(row_number, strips, v0, basis0, basis_rows, near_rows)
    left, m, basis_m = panel1(
        row_number, rest_all, strips, v0, basis0, basis_rows, left_feat, right_feat, near_rows,
        left0,
    )
    place = jnp.stack([my_row, my_col]).astype(jnp.int32)
    return trailing(
        place, cols_all.reshape(NX, NZ, 384, TILE), near_cols, base, left, m, basis_m
    )


def solution(mesh):
    in_specs = (P(None, BOTH), P("row", None), P("row", "col"))
    out_specs = P("row", "col")
    return jax.shard_map(local, mesh=mesh, in_specs=in_specs, out_specs=out_specs, check_vma=False)
```

```python
import jax
import jax.numpy as jnp
from jax import lax
from jax.experimental import pallas as pl
from jax.experimental.pallas import tpu as pltpu
from jax.sharding import PartitionSpec as P

TILE = 128
PANEL = 512
FIRST = 1024
BLOCK = 16
NX, NZ, NC = 4, 8, 8

nugget = 0.5
range_cells = 3.0
highest = lax.Precision.HIGHEST
BOTH = ("row", "col")


def dot_nn(a, b):
    return lax.dot_general(
        a, b, (((1,), (0,)), ((), ())), precision=highest, preferred_element_type=jnp.float32
    )


def dot_nt(a, b):
    return lax.dot_general(
        a, b, (((1,), (1,)), ((), ())), precision=highest, preferred_element_type=jnp.float32
    )


def dot_tn(a, b):
    return lax.dot_general(
        a, b, (((0,), (0,)), ((), ())), precision=highest, preferred_element_type=jnp.float32
    )


def times_lower_t(a, v):
    half = v.shape[0] // 2
    return jnp.concatenate([dot_nt(a[:, :half], v[:half, :half]), dot_nt(a, v[half:, :])], axis=1)


def times_lower(a, v):
    half = v.shape[0] // 2
    return jnp.concatenate([dot_nn(a, v[:, :half]), dot_nn(a[:, half:], v[half:, half:])], axis=1)


def near_dot(a, b):
    return jnp.exp(jnp.sqrt(jnp.maximum(dot_tn(a, b), 0.0)) * (-1.0 / range_cells))


def reciprocal(x):
    r = pl.reciprocal(x, approx=True)
    return r * (2.0 - x * r)


def bf16_parts(v):
    high = v.astype(jnp.bfloat16)
    rest = v - high.astype(jnp.float32)
    mid = rest.astype(jnp.bfloat16)
    return high, mid, (rest - mid.astype(jnp.float32)).astype(jnp.bfloat16)


def stacked_dot(a, b, a_dim):
    a1, a2, a3 = bf16_parts(a)
    b1, b2, b3 = bf16_parts(b)
    left = jnp.concatenate([a3, a1, a2, a2, a1, a1], axis=a_dim)
    right = jnp.concatenate([b1, b3, b2, b1, b2, b1], axis=0)
    return lax.dot_general(
        left, right, (((a_dim,), (0,)), ((), ())), preferred_element_type=jnp.float32
    )


def eliminate(p, x, k):
    groups = p.shape[0] // 8
    sub = lax.broadcasted_iota(jnp.int32, (8, TILE), 0)

    def row(v, q):
        return jnp.broadcast_to(v[q // 8][q % 8 : q % 8 + 1], (8, TILE))

    p = [p[8 * g : 8 * g + 8] for g in range(groups)]
    x = [x[8 * g : 8 * g + 8] for g in range(groups)]
    cols = [
        [jnp.broadcast_to(p[g][:, k + q : k + q + 1], (8, TILE)) for g in range(groups)]
        for q in range(BLOCK)
    ]
    pivots = [jnp.zeros((8, TILE), jnp.float32) for _ in range(BLOCK // 8)]
    for q in range(0, BLOCK, 2):
        first, second = cols[q], cols[q + 1]
        a, b, d = row(first, q), row(second, q), row(second, q + 1)
        det = a * d - b * b
        r1, r2 = reciprocal(a), reciprocal(det)
        top, lo = q // 8, q % 8
        pivots[top] = jnp.where(sub == lo, a, jnp.where(sub == lo + 1, det * r1, pivots[top]))
        m1, m2 = [None] * groups, [None] * groups
        for g in range(top, groups):
            m1[g] = (d * first[g] - b * second[g]) * r2
            m2[g] = (a * second[g] - b * first[g]) * r2
            if g == top:
                m1[g] = jnp.where(sub > lo + 1, m1[g], jnp.where(sub == lo + 1, b * r1, 0.0))
                m2[g] = jnp.where(sub > lo + 1, m2[g], 0.0)
        for s in range(q + 2, BLOCK):
            u, v = row(cols[s], q), row(cols[s], q + 1)
            for g in range((q + 2) // 8, groups):
                cols[s][g] = cols[s][g] - m1[g] * u - m2[g] * v
        for w in (p, x):
            u, v = row(w, q), row(w, q + 1)
            for g in range(top, groups):
                w[g] = w[g] - m1[g] * u - m2[g] * v
    return jnp.concatenate(p, 0), jnp.concatenate(x, 0), jnp.concatenate(pivots, 0)


def factor_tile(t):
    row = lax.broadcasted_iota(jnp.int32, (TILE, TILE), 0)
    lane = lax.broadcasted_iota(jnp.int32, (TILE, TILE), 1)
    eye = jnp.where(row == lane, 1.0, 0.0).astype(jnp.float32)
    blocks = TILE // BLOCK
    ts = [t[b * BLOCK : (b + 1) * BLOCK] for b in range(blocks)]
    ws = [eye[b * BLOCK : (b + 1) * BLOCK] for b in range(blocks)]
    uppers, inverses = [], []
    for b in range(blocks):
        last = b + 1 == blocks
        both = slice(b, b + 1) if last else slice(b, b + 2)
        p, x, pivots = eliminate(
            jnp.concatenate(ts[both], 0), jnp.concatenate(ws[both], 0), b * BLOCK
        )
        scale = lax.rsqrt(pivots)
        uppers.append(p[:BLOCK] * scale)
        inverses.append(x[:BLOCK] * scale)
        if not last:
            ts[b + 1], ws[b + 1] = p[BLOCK:], x[BLOCK:]
        if b + 2 < blocks:
            prod = stacked_dot(
                uppers[b], jnp.concatenate([uppers[b], inverses[b]], axis=1), 0
            )
            for c in range(b + 2, blocks):
                rows = slice(c * BLOCK, (c + 1) * BLOCK)
                ts[c] = ts[c] - prod[rows, :TILE]
                ws[c] = ws[c] - prod[rows, TILE:]
    u = jnp.where(lane >= row, jnp.concatenate(uppers, 0), 0.0)
    return u, jnp.concatenate(inverses, 0)


def factor_in_place(work, tiles):
    n = tiles * TILE
    for j in range(tiles):
        rows = slice(j * TILE, (j + 1) * TILE)
        u, v = factor_tile(work[rows, rows])
        live = slice((j + 1) * TILE, n + j * TILE)
        work[rows, live] = stacked_dot(v, work[rows, live], 1)
        work[rows, rows] = u
        work[rows, n + j * TILE : n + (j + 1) * TILE] = v
        below = slice((j + 1) * TILE, n)
        if j + 1 < tiles:
            wide = slice((j + 1) * TILE, n + (j + 1) * TILE)
            work[below, wide] = work[below, wide] - stacked_dot(
                work[rows, below], work[rows, wide], 0
            )


def add_nugget(work):
    row = lax.broadcasted_iota(jnp.int32, (TILE, TILE), 0)
    lane = lax.broadcasted_iota(jnp.int32, (TILE, TILE), 1)
    diagonal = jnp.where(row == lane, nugget, 0.0).astype(jnp.float32)
    for z in range(4):
        rows = slice(z * TILE, (z + 1) * TILE)
        work[rows, rows] = work[rows, rows] + diagonal


def global_rows(place, width):
    row = lax.broadcasted_iota(jnp.int32, (256, width), 0)
    return jnp.where(row < TILE, row + place[0] * TILE, row + (place[0] + 31) * TILE)


def keep_lower(value, place, start):
    lane = lax.broadcasted_iota(jnp.int32, (256, PANEL), 1)
    return jnp.where(global_rows(place, PANEL) - start >= lane, value, 0.0)


def place_basis(part, offset, basis):
    for c in range(NC):
        for z in range(4):
            for l in range(4):
                basis[z * TILE + c * 16 : z * TILE + c * 16 + 16, l * TILE : (l + 1) * TILE] = (
                    part(c, z)[offset + l * 16 : offset + l * 16 + 16, :]
                )


def extra_rows(part, offset, first):
    halves = []
    for z in range(first, first + 2):
        for h in range(2):
            halves.append(
                jnp.concatenate(
                    [part(h * 4 + q, z)[offset : offset + 64, :] for q in range(4)], axis=1
                )
            )
    return jnp.concatenate(halves, axis=0)


def site_tile(pieces):
    value = pieces[0]
    for j in range(1, 4):
        value = value + pltpu.roll(pieces[j], 32 * j, 1)
    return value


def fetch(pairs, sems):
    copies = [pltpu.make_async_copy(a, b, sems.at[i]) for i, (a, b) in enumerate(pairs)]
    for copy in copies:
        copy.start()
    return copies


def near_rows(place, row_feat, right_feat, start):
    near = near_dot(row_feat[:8, :], right_feat[8:, start : start + PANEL])
    lane = lax.broadcasted_iota(jnp.int32, (256, PANEL), 1)
    return near + jnp.where(global_rows(place, PANEL) - start == lane, nugget, 0.0)


def panel0_kernel(
    place, own0, own1, own2, own3, other0, other1, other2, other3, strips, basis_rows,
    v_out, basis_out, left_out, feat_out,
    parts, strip, phi, basis, left0, feat, row_feat, work, sems, out_sems,
):
    core, y = place[1] % 2, place[1] // 2
    pairs = [
        (piece, parts.at[k, (y + 4 - shift) % 4])
        for k, pieces in ((core, (own0, own1, own2, own3)), (1 - core, (other0, other1, other2, other3)))
        for shift, piece in enumerate(pieces)
    ]
    copies = fetch(pairs + [(strips, strip), (basis_rows, phi)], sems)
    work[:, PANEL:] = jnp.zeros((PANEL, PANEL), jnp.float32)
    for copy in copies[:8]:
        copy.wait()

    def part(c, z):
        return parts.at[c % 2, c // 2, z]

    place_basis(part, 64, basis)
    for z in range(4):
        for h in range(2):
            pieces = [part(4 * h + j, z)[128:144, :] for j in range(4)]
            feat[:, (2 * z + h) * TILE : (2 * z + h + 1) * TILE] = site_tile(pieces)
    outs = [
        pltpu.make_async_copy(basis, basis_out, out_sems.at[0]),
        pltpu.make_async_copy(feat, feat_out, out_sems.at[1]),
        pltpu.make_async_copy(work.at[:, pl.ds(PANEL, PANEL)], v_out, out_sems.at[2]),
        pltpu.make_async_copy(left0, left_out, out_sems.at[3]),
    ]
    outs[0].start()
    outs[1].start()
    for z in range(0, 4, 2):
        rows = slice(z * TILE, (z + 2) * TILE)
        near = near_dot(feat[:8, rows], feat[8:, :PANEL])
        work[rows, :PANEL] = extra_rows(part, 0, z) + near + dot_nt(basis[rows, :], basis[...])
    add_nugget(work)
    factor_in_place(work, 4)
    outs[2].start()
    for copy in copies[8:]:
        copy.wait()
    extra = jnp.concatenate([strip[q, :256, :] for q in range(4)], axis=1)
    for h in range(2):
        pieces = [strip[4 * h + j, 256:272, :] for j in range(4)]
        row_feat[:, h * TILE : (h + 1) * TILE] = site_tile(pieces)
    a = extra + near_rows(place, row_feat, feat, 0) + dot_nt(phi[...], basis[...])
    left0[...] = keep_lower(times_lower_t(a, work[:, PANEL:]), place, 0)
    outs[3].start()
    for copy in outs:
        copy.wait()


def panel1_kernel(
    place, rest, strips, v0_in, basis0_in, basis_rows, left0_in, feat_in,
    left_out, m_out, basis_m_out,
    parts, strip, v0, basis0, phi, left0, feat, row_feat, work, basis1, l10, left1, m, basis_m,
    sems, out_sems,
):
    copies = fetch(
        [
            (rest, parts),
            (basis0_in, basis0),
            (v0_in, v0),
            (strips, strip),
            (basis_rows, phi),
            (left0_in, left0),
            (feat_in, feat),
        ],
        sems,
    )
    work[:, PANEL:] = jnp.zeros((PANEL, PANEL), jnp.float32)
    for copy in copies:
        copy.wait()

    def part(c, z):
        return parts.at[c, z]

    place_basis(part, 64, basis1)
    for z in range(0, 4, 2):
        rows = slice(z * TILE, (z + 2) * TILE)
        near = near_dot(feat[:8, PANEL + z * TILE : PANEL + (z + 2) * TILE], feat[8:, :])
        a10 = extra_rows(part, 0, z) + near[:, :PANEL] + dot_nt(basis1[rows, :], basis0[...])
        l10[rows, :] = times_lower_t(a10, v0[...])
        work[rows, :PANEL] = extra_rows(part, 128, z) + near[:, PANEL:]
    for z in range(0, 4, 2):
        rows = slice(z * TILE, (z + 2) * TILE)
        cols = slice(z * TILE, PANEL)
        work[rows, cols] = (
            work[rows, cols]
            + dot_nt(basis1[rows, :], basis1[cols, :])
            - dot_nt(l10[rows, :], l10[cols, :])
        )
    add_nugget(work)
    for h in range(2):
        pieces = [strip[4 * h + j, 256:272, :] for j in range(4)]
        row_feat[:, h * TILE : (h + 1) * TILE] = site_tile(pieces)
    extra = jnp.concatenate([strip[4 + q, :256, :] for q in range(4)], axis=1)
    left1[...] = (
        extra
        + near_rows(place, row_feat, feat, PANEL)
        + dot_nt(phi[...], basis1[...])
        - dot_nt(left0[...], l10[...])
    )
    factor_in_place(work, 4)
    v1 = work[:, PANEL:]
    left1[...] = keep_lower(times_lower_t(left1[...], v1), place, PANEL)
    outs = [
        pltpu.make_async_copy(left0, left_out.at[0], out_sems.at[0]),
        pltpu.make_async_copy(left1, left_out.at[1], out_sems.at[1]),
        pltpu.make_async_copy(m, m_out, out_sems.at[2]),
        pltpu.make_async_copy(basis_m, basis_m_out, out_sems.at[3]),
    ]
    outs[0].start()
    outs[1].start()
    m1 = times_lower(left1[...], v1)
    m0 = times_lower(left0[...] - dot_nn(m1, l10[...]), v0[...])
    m[:, :PANEL] = m0
    m[:, PANEL:] = m1
    outs[2].start()
    basis_m[...] = phi[...] - dot_nn(m0, basis0[...]) - dot_nn(m1, basis1[...])
    outs[3].start()
    for copy in outs:
        copy.wait()


def trailing_kernel(
    place, cols_in, strips, extra_in, left_in, m_in, basis_m_in, feat_in,
    out,
    cols, strip, extra, left, m, basis_m, feat, row_feat, result, sems, col_sems, out_sems,
):
    copies = fetch(
        [
            (m_in, m),
            (basis_m_in, basis_m),
            (feat_in, feat),
            (strips.at[:, pl.ds(256, 16), :], strip),
            (extra_in, extra),
            (left_in, left),
        ],
        sems,
    )

    def col_copy(x):
        return pltpu.make_async_copy(cols_in.at[x], cols.at[x], col_sems.at[x])

    def out_copy(tile):
        lanes = pl.ds(pl.multiple_of(tile * TILE, TILE), TILE)
        return pltpu.make_async_copy(result.at[:, lanes], out.at[:, lanes], out_sems.at[tile])

    for x in range(NX):
        col_copy(x).start()
    for copy in copies:
        copy.wait()
    for h in range(2):
        row_feat[:, h * TILE : (h + 1) * TILE] = site_tile([strip[4 * h + j] for j in range(4)])
    row = lax.broadcasted_iota(jnp.int32, (256, TILE), 0)
    lane = lax.broadcasted_iota(jnp.int32, (256, TILE), 1)
    zero = (row < TILE) & (place[0] < 8)
    row_global = global_rows(place, TILE)

    def step(x, carry):
        col_copy(x).wait()
        col_feat = jnp.concatenate(
            [site_tile([cols[x, 4 * h + j, 384:400, :] for j in range(4)]) for h in range(2)],
            axis=1,
        )
        cross = jnp.concatenate([cols[x, c, :256, :] for c in range(NC)], axis=1)
        cross = cross + near_dot(col_feat[:8], feat[8:, :])
        basis_c = jnp.concatenate(
            [
                jnp.concatenate(
                    [cols[x, c, 256 + l * 32 : 288 + l * 32, :] for l in range(4)], axis=1
                )
                for c in range(NC)
            ],
            axis=0,
        )
        value = near_dot(row_feat[:8, :], col_feat[8:])
        value = value + dot_nt(basis_m[...], basis_c) - dot_nt(m[...], cross)
        for h in range(2):
            tile = h * 4 + x
            lanes = pl.ds(pl.multiple_of(tile * TILE, TILE), TILE)
            same = row_global == (tile * 8 + place[1]) * TILE + lane
            part = value[:, h * TILE : (h + 1) * TILE] + extra[:, lanes]
            result[:, lanes] = jnp.where(zero, 0.0, part + jnp.where(same, nugget, 0.0))

        @pl.when(x == 0)
        def _():
            own = pl.ds(pl.multiple_of(place[1] % 4 * TILE, TILE), TILE)
            result[:, :TILE] = left[place[1] // 4, :, own]

        out_copy(x).start()
        out_copy(x + 4).start()
        return carry

    lax.fori_loop(0, NX, step, 0)
    for tile in range(8):
        out_copy(tile).wait()


SMEM = pl.BlockSpec(memory_space=pltpu.SMEM)
HBM = pl.BlockSpec(memory_space=pltpu.HBM)


def call(kernel, place, inputs, outs, scratch, sems, us):
    return pl.pallas_call(
        kernel,
        out_shape=[jax.ShapeDtypeStruct(shape, jnp.float32) for shape in outs],
        in_specs=[SMEM] + [HBM] * len(inputs),
        out_specs=[HBM] * len(outs),
        scratch_shapes=[pltpu.VMEM(shape, jnp.float32) for shape in scratch]
        + [pltpu.SemaphoreType.DMA((n,)) for n in sems],
        compiler_params=pltpu.CompilerParams(vmem_limit_bytes=58 * 2**20),
        cost_estimate=pl.CostEstimate(
            flops=us * 10**9, bytes_accessed=us * 3 * 10**6, transcendentals=0
        ),
    )(place, *inputs)


SQUARE, ROWS, FEAT = (PANEL, PANEL), (256, PANEL), (16, FIRST)
WORK, STRIPS = (PANEL, 2 * PANEL), (NC, 272, TILE)


def panel0(place, *inputs):
    outs = [SQUARE, SQUARE, ROWS, FEAT]
    scratch = [(2, 4, 4, 144, TILE), STRIPS, ROWS, SQUARE, ROWS, FEAT, (16, 256), WORK]
    return call(panel0_kernel, place, inputs, outs, scratch, (10, 4), 30)


def panel1(place, *inputs):
    outs = [(2, 256, PANEL), (256, FIRST), ROWS]
    scratch = [
        (NC, 4, 192, TILE), STRIPS, SQUARE, SQUARE, ROWS, ROWS, FEAT, (16, 256), WORK,
        SQUARE, SQUARE, ROWS, (256, FIRST), ROWS,
    ]
    return call(panel1_kernel, place, inputs, outs, scratch, (7, 4), 40)


def trailing(place, *inputs):
    scratch = [
        (NX, NZ, 400, TILE), (NC, 16, TILE), (256, FIRST), (2, 256, PANEL), (256, FIRST), ROWS,
        FEAT, (16, 256), (256, FIRST),
    ]
    return call(trailing_kernel, place, inputs, [(256, FIRST)], scratch, (6, 4, 8), 10)[0]


def spread_to(value, axis, count, groups=None):
    every = jnp.broadcast_to(value[None], (count,) + value.shape)
    return lax.all_to_all(every, axis, 0, 0, axis_index_groups=groups)


def after(value, done):
    return jnp.where(done == done, value, jnp.zeros_like(value))


def lane_groups(rows):
    n = rows.shape[0]
    return rows.reshape(n, 4, TILE).transpose(1, 0, 2).reshape(4 * n, TILE)


def local(site_coords, basis_rows, extra_cov):
    my_row = lax.axis_index("row")
    my_col = lax.axis_index("col")
    place = jnp.stack([my_row, my_col]).astype(jnp.int32)
    z_groups = [[x * NZ + z for z in range(NZ)] for x in range(NX)]
    places = [(x, z, c) for x in range(NX) for z in range(NZ) for c in range(NC)]
    strip = extra_cov[:, :TILE]

    sites = site_coords.astype(jnp.float32)
    square = jnp.sum(sites * sites, axis=0, keepdims=True)
    one, none = jnp.ones((1, 32), jnp.float32), jnp.zeros((3, 32), jnp.float32)
    own_feat = jnp.concatenate([sites, square, one, none, -2.0 * sites, one, square, none])
    own_feat = jnp.pad(own_feat, ((0, 0), (0, 96)))

    def piece_of(r, c):
        return 4 * r + c % 4 + 128 * (c // 4)

    to_rows = [(piece_of(x * NZ + z, c), (x * NZ + z) * NC + c) for x, z, c in places]
    to_cols = [(piece_of(x * NZ + c, z), (x * NZ + z) * NC + c) for x, z, c in places]
    row_piece = lax.ppermute(own_feat, BOTH, to_rows)
    col_piece = lax.ppermute(own_feat, BOTH, to_cols)

    turn = [((x * NZ + z) * NC + c, (x * NZ + c) * NC + z) for x, z, c in places]
    basis_part = lane_groups(lax.dynamic_slice_in_dim(basis_rows, my_col * 32, 32, 0))
    turned = lax.ppermute(jnp.concatenate([strip, basis_part]), BOTH, turn)

    half = my_col // 4
    packs = []
    for h in range(2):
        piece = (my_col % 4 + 4 * h) * 16
        basis_16 = lane_groups(lax.dynamic_slice_in_dim(basis_rows, piece, 16, 0))
        basis_8 = lax.dynamic_slice_in_dim(basis_16, half * 32, 32, 0)
        packs.append(jnp.concatenate([strip[h * 64 : h * 64 + 64], basis_8, own_feat]))
    x_groups = [
        [(x * NZ + z) * NC + q + 4 * h for x in range(NX) for h in range(2)]
        for z in range(NZ)
        for q in range(4)
    ]
    pair = jnp.concatenate(packs).reshape(1, 2, 112, TILE)
    pair = jnp.broadcast_to(pair, (NX, 2, 112, TILE)).reshape(2 * NX, 112, TILE)
    over_x = lax.all_to_all(pair, BOTH, 0, 0, axis_index_groups=x_groups)
    first_of = jnp.where(half == 0, over_x[0, 96:], over_x[1, 96:])
    pack = jnp.concatenate(
        [over_x[0, :64], over_x[0, 64:96], over_x[1, 64:96], first_of, over_x[1, :64]]
    )
    over_z = spread_to(after(pack, turned[0, 0]), "row", NZ, z_groups)

    panel_part = over_z[:4, :144]
    owns = [panel_part] + [
        lax.ppermute(panel_part, "col", [(c, (c + 2 * k) % NC) for c in range(NC)])
        for k in range(1, 4)
    ]
    others = [lax.ppermute(own, "col", [(c, c ^ 1) for c in range(NC)]) for own in owns]
    rest = jnp.concatenate([over_z[4:, :128], over_z[4:, 144:]], axis=1)
    rest_all = spread_to(after(rest, owns[2][0, 0, 0]), "col", NC)

    strips = lax.all_gather(jnp.concatenate([strip, row_piece]), "col", axis=0)
    for_cols = after(jnp.concatenate([turned, col_piece]), over_z[0, 0, 0])
    cols_all = lax.all_gather(for_cols, "row", axis=0).reshape(NX, NZ, 400, TILE)

    v0, basis0, left0, feat = panel0(place, *owns, *others, strips, basis_rows)
    left, m, basis_m = panel1(place, rest_all, strips, v0, basis0, basis_rows, left0, feat)
    return trailing(place, cols_all, strips, extra_cov, left, m, basis_m, feat)


def solution(mesh):
    in_specs = (P(None, BOTH), P("row", None), P("row", "col"))
    out_specs = P("row", "col")
    return jax.shard_map(local, mesh=mesh, in_specs=in_specs, out_specs=out_specs, check_vma=False)
```

```python
import jax
import jax.numpy as jnp
from jax import lax
from jax.experimental import pallas as pl
from jax.experimental.pallas import tpu as pltpu
from jax.sharding import PartitionSpec as P

TILE = 128
PANEL = 512
FIRST = 1024
BLOCK = 16
NX, NZ, NC = 4, 8, 8

nugget = 0.5
range_cells = 3.0
highest = lax.Precision.HIGHEST
BOTH = ("row", "col")


def dot_nn(a, b):
    return lax.dot_general(
        a, b, (((1,), (0,)), ((), ())), precision=highest, preferred_element_type=jnp.float32
    )


def dot_nt(a, b):
    return lax.dot_general(
        a, b, (((1,), (1,)), ((), ())), precision=highest, preferred_element_type=jnp.float32
    )


def dot_tn(a, b):
    return lax.dot_general(
        a, b, (((0,), (0,)), ((), ())), precision=highest, preferred_element_type=jnp.float32
    )


def times_lower_t(a, v):
    half = v.shape[0] // 2
    return jnp.concatenate([dot_nt(a[:, :half], v[:half, :half]), dot_nt(a, v[half:, :])], axis=1)


def times_lower(a, v):
    half = v.shape[0] // 2
    return jnp.concatenate([dot_nn(a, v[:, :half]), dot_nn(a[:, half:], v[half:, half:])], axis=1)


def near_dot(a, b):
    return jnp.exp(jnp.sqrt(jnp.maximum(dot_tn(a, b), 0.0)) * (-1.0 / range_cells))


def reciprocal(x):
    r = pl.reciprocal(x, approx=True)
    return r * (2.0 - x * r)


def bf16_parts(v):
    high = v.astype(jnp.bfloat16)
    rest = v - high.astype(jnp.float32)
    mid = rest.astype(jnp.bfloat16)
    return high, mid, (rest - mid.astype(jnp.float32)).astype(jnp.bfloat16)


def stacked_dot(a, b, a_dim):
    a1, a2, a3 = bf16_parts(a)
    b1, b2, b3 = bf16_parts(b)
    left = jnp.concatenate([a3, a1, a2, a2, a1, a1], axis=a_dim)
    right = jnp.concatenate([b1, b3, b2, b1, b2, b1], axis=0)
    return lax.dot_general(
        left, right, (((a_dim,), (0,)), ((), ())), preferred_element_type=jnp.float32
    )


def eliminate(p, x, k):
    groups = p.shape[0] // 8
    sub = lax.broadcasted_iota(jnp.int32, (8, TILE), 0)

    def row(v, q):
        return jnp.broadcast_to(v[q // 8][q % 8 : q % 8 + 1], (8, TILE))

    p = [p[8 * g : 8 * g + 8] for g in range(groups)]
    x = [x[8 * g : 8 * g + 8] for g in range(groups)]
    cols = [
        [jnp.broadcast_to(p[g][:, k + q : k + q + 1], (8, TILE)) for g in range(groups)]
        for q in range(BLOCK)
    ]
    pivots = [jnp.zeros((8, TILE), jnp.float32) for _ in range(BLOCK // 8)]
    for q in range(0, BLOCK, 2):
        first, second = cols[q], cols[q + 1]
        a, b, d = row(first, q), row(second, q), row(second, q + 1)
        det = a * d - b * b
        r1, r2 = reciprocal(a), reciprocal(det)
        top, lo = q // 8, q % 8
        pivots[top] = jnp.where(sub == lo, a, jnp.where(sub == lo + 1, det * r1, pivots[top]))
        m1, m2 = [None] * groups, [None] * groups
        for g in range(top, groups):
            m1[g] = (d * first[g] - b * second[g]) * r2
            m2[g] = (a * second[g] - b * first[g]) * r2
            if g == top:
                m1[g] = jnp.where(sub > lo + 1, m1[g], jnp.where(sub == lo + 1, b * r1, 0.0))
                m2[g] = jnp.where(sub > lo + 1, m2[g], 0.0)
        for s in range(q + 2, BLOCK):
            u, v = row(cols[s], q), row(cols[s], q + 1)
            for g in range((q + 2) // 8, groups):
                cols[s][g] = cols[s][g] - m1[g] * u - m2[g] * v
        for w in (p, x):
            u, v = row(w, q), row(w, q + 1)
            for g in range(top, groups):
                w[g] = w[g] - m1[g] * u - m2[g] * v
    return jnp.concatenate(p, 0), jnp.concatenate(x, 0), jnp.concatenate(pivots, 0)


def factor_tile(t):
    row = lax.broadcasted_iota(jnp.int32, (TILE, TILE), 0)
    lane = lax.broadcasted_iota(jnp.int32, (TILE, TILE), 1)
    eye = jnp.where(row == lane, 1.0, 0.0).astype(jnp.float32)
    blocks = TILE // BLOCK
    ts = [t[b * BLOCK : (b + 1) * BLOCK] for b in range(blocks)]
    ws = [eye[b * BLOCK : (b + 1) * BLOCK] for b in range(blocks)]
    uppers, inverses = [], []
    for b in range(blocks):
        last = b + 1 == blocks
        both = slice(b, b + 1) if last else slice(b, b + 2)
        p, x, pivots = eliminate(
            jnp.concatenate(ts[both], 0), jnp.concatenate(ws[both], 0), b * BLOCK
        )
        scale = lax.rsqrt(pivots)
        uppers.append(p[:BLOCK] * scale)
        inverses.append(x[:BLOCK] * scale)
        if not last:
            ts[b + 1], ws[b + 1] = p[BLOCK:], x[BLOCK:]
        if b + 2 < blocks:
            prod = stacked_dot(
                uppers[b], jnp.concatenate([uppers[b], inverses[b]], axis=1), 0
            )
            for c in range(b + 2, blocks):
                rows = slice(c * BLOCK, (c + 1) * BLOCK)
                ts[c] = ts[c] - prod[rows, :TILE]
                ws[c] = ws[c] - prod[rows, TILE:]
    u = jnp.where(lane >= row, jnp.concatenate(uppers, 0), 0.0)
    return u, jnp.concatenate(inverses, 0)


def factor_in_place(work, tiles):
    n = tiles * TILE
    for j in range(tiles):
        rows = slice(j * TILE, (j + 1) * TILE)
        u, v = factor_tile(work[rows, rows])
        live = slice((j + 1) * TILE, n + j * TILE)
        work[rows, live] = stacked_dot(v, work[rows, live], 1)
        work[rows, rows] = u
        work[rows, n + j * TILE : n + (j + 1) * TILE] = v
        below = slice((j + 1) * TILE, n)
        if j + 1 < tiles:
            wide = slice((j + 1) * TILE, n + (j + 1) * TILE)
            work[below, wide] = work[below, wide] - stacked_dot(
                work[rows, below], work[rows, wide], 0
            )


def add_nugget(work):
    row = lax.broadcasted_iota(jnp.int32, (TILE, TILE), 0)
    lane = lax.broadcasted_iota(jnp.int32, (TILE, TILE), 1)
    diagonal = jnp.where(row == lane, nugget, 0.0).astype(jnp.float32)
    for z in range(4):
        rows = slice(z * TILE, (z + 1) * TILE)
        work[rows, rows] = work[rows, rows] + diagonal


def global_rows(place, width):
    row = lax.broadcasted_iota(jnp.int32, (256, width), 0)
    return jnp.where(row < TILE, row + place[0] * TILE, row + (place[0] + 31) * TILE)


def keep_lower(value, place, start):
    lane = lax.broadcasted_iota(jnp.int32, (256, PANEL), 1)
    return jnp.where(global_rows(place, PANEL) - start >= lane, value, 0.0)


def place_basis(part, basis):
    for c in range(NC):
        for z in range(4):
            for l in range(4):
                basis[z * TILE + c * 16 : z * TILE + c * 16 + 16, l * TILE : (l + 1) * TILE] = (
                    part(c, z, l)[16:32, :]
                )


def extra_rows(part, offset, first):
    return jnp.concatenate(
        [
            jnp.concatenate(
                [part(h * 4 + q, z, x)[offset : offset + 16, :] for q in range(4)], axis=1
            )
            for z in range(first, first + 2)
            for h in range(2)
            for x in range(NX)
        ],
        axis=0,
    )


def slots(place):
    return [(place[0] // NZ + 4 - x) % 4 for x in range(NX)]


def site_tile(pieces):
    value = pieces[0]
    for j in range(1, 4):
        value = value + pltpu.roll(pieces[j], 32 * j, 1)
    return value


def fetch(pairs, sems):
    copies = [pltpu.make_async_copy(a, b, sems.at[i]) for i, (a, b) in enumerate(pairs)]
    for copy in copies:
        copy.start()
    return copies


def near_rows(place, row_feat, right_feat, start):
    near = near_dot(row_feat[:8, :], right_feat[8:, start : start + PANEL])
    lane = lax.broadcasted_iota(jnp.int32, (256, PANEL), 1)
    return near + jnp.where(global_rows(place, PANEL) - start == lane, nugget, 0.0)


def from_cols(place, parts, owns, others):
    core, y = place[1] % 2, place[1] // 2
    return [
        (piece, parts.at[k, (y + 4 - shift) % 4])
        for k, pieces in ((core, owns), (1 - core, others))
        for shift, piece in enumerate(pieces)
    ]


def panel0_kernel(
    place, own0, own1, own2, own3, other0, other1, other2, other3, strips, basis_rows,
    v_out, basis_out, left_out, feat_out, row_out,
    parts, strip, phi, basis, left0, feat, row_feat, work, sems, out_sems,
):
    pairs = from_cols(place, parts, (own0, own1, own2, own3), (other0, other1, other2, other3))
    copies = fetch(pairs + [(strips, strip), (basis_rows, phi)], sems)
    work[:, PANEL:] = jnp.zeros((PANEL, PANEL), jnp.float32)
    for copy in copies[:8]:
        copy.wait()

    slot = slots(place)

    def part(c, z, x):
        return parts.at[c % 2, c // 2, slot[x], z]

    place_basis(part, basis)
    for z in range(4):
        for h in range(2):
            lanes = slice((2 * z + h) * TILE, (2 * z + h + 1) * TILE)
            for side in range(2):
                pieces = [part(4 * h + j, z, side)[32:40, :] for j in range(4)]
                feat[side * 8 : side * 8 + 8, lanes] = site_tile(pieces)
    outs = [
        pltpu.make_async_copy(basis, basis_out, out_sems.at[0]),
        pltpu.make_async_copy(feat, feat_out, out_sems.at[1]),
        pltpu.make_async_copy(work.at[:, pl.ds(PANEL, PANEL)], v_out, out_sems.at[2]),
        pltpu.make_async_copy(left0, left_out, out_sems.at[3]),
        pltpu.make_async_copy(row_feat, row_out, out_sems.at[4]),
    ]
    outs[0].start()
    outs[1].start()
    for z in range(0, 4, 2):
        rows = slice(z * TILE, (z + 2) * TILE)
        near = near_dot(feat[:8, rows], feat[8:, :PANEL])
        work[rows, :PANEL] = extra_rows(part, 0, z) + near + dot_nt(basis[rows, :], basis[...])
    add_nugget(work)
    factor_in_place(work, 4)
    outs[2].start()
    for copy in copies[8:]:
        copy.wait()
    for h in range(2):
        pieces = [strip[4 * h + j, 256:272, :] for j in range(4)]
        row_feat[:, h * TILE : (h + 1) * TILE] = site_tile(pieces)
    outs[4].start()
    extra = jnp.concatenate([strip[q, :256, :] for q in range(4)], axis=1)
    a = extra + near_rows(place, row_feat, feat, 0) + dot_nt(phi[...], basis[...])
    left0[...] = keep_lower(times_lower_t(a, work[:, PANEL:]), place, 0)
    outs[3].start()
    for copy in outs:
        copy.wait()


def panel1_kernel(
    place, own0, own1, own2, own3, other0, other1, other2, other3, strips, v0_in, basis0_in,
    basis_rows, left0_in, feat_in, row_in,
    left_out, m_out, basis_m_out,
    parts, strip, v0, basis0, phi, left0, feat, row_feat, work, basis1, l10, left1, m, basis_m,
    sems, out_sems,
):
    pairs = from_cols(place, parts, (own0, own1, own2, own3), (other0, other1, other2, other3))
    copies = fetch(
        pairs
        + [
            (feat_in, feat),
            (basis0_in, basis0),
            (v0_in, v0),
            (strips.at[pl.ds(4, 4), pl.ds(0, 256), :], strip),
            (basis_rows, phi),
            (left0_in, left0),
            (row_in, row_feat),
        ],
        sems,
    )
    work[:, PANEL:] = jnp.zeros((PANEL, PANEL), jnp.float32)
    for copy in copies[:9]:
        copy.wait()
    slot = slots(place)

    def part(c, z, x):
        return parts.at[c % 2, c // 2, slot[x], z]

    place_basis(part, basis1)
    for z in range(0, 4, 2):
        rows = slice(z * TILE, (z + 2) * TILE)
        near = near_dot(feat[:8, PANEL + z * TILE : PANEL + (z + 2) * TILE], feat[8:, :])
        l10[rows, :] = extra_rows(part, 0, z) + near[:, :PANEL]
        work[rows, :PANEL] = extra_rows(part, 32, z) + near[:, PANEL:]
    for copy in copies[9:]:
        copy.wait()
    for z in range(0, 4, 2):
        rows = slice(z * TILE, (z + 2) * TILE)
        a10 = l10[rows, :] + dot_nt(basis1[rows, :], basis0[...])
        l10[rows, :] = times_lower_t(a10, v0[...])
    for z in range(0, 4, 2):
        rows = slice(z * TILE, (z + 2) * TILE)
        cols = slice(z * TILE, PANEL)
        work[rows, cols] = (
            work[rows, cols]
            + dot_nt(basis1[rows, :], basis1[cols, :])
            - dot_nt(l10[rows, :], l10[cols, :])
        )
    add_nugget(work)
    extra = jnp.concatenate([strip[q] for q in range(4)], axis=1)
    left1[...] = (
        extra
        + near_rows(place, row_feat, feat, PANEL)
        + dot_nt(phi[...], basis1[...])
        - dot_nt(left0[...], l10[...])
    )
    factor_in_place(work, 4)
    v1 = work[:, PANEL:]
    left1[...] = keep_lower(times_lower_t(left1[...], v1), place, PANEL)
    outs = [
        pltpu.make_async_copy(left0, left_out.at[0], out_sems.at[0]),
        pltpu.make_async_copy(left1, left_out.at[1], out_sems.at[1]),
        pltpu.make_async_copy(m, m_out, out_sems.at[2]),
        pltpu.make_async_copy(basis_m, basis_m_out, out_sems.at[3]),
    ]
    outs[0].start()
    outs[1].start()
    m1 = times_lower(left1[...], v1)
    m0 = times_lower(left0[...] - dot_nn(m1, l10[...]), v0[...])
    m[:, :PANEL] = m0
    m[:, PANEL:] = m1
    outs[2].start()
    basis_m[...] = phi[...] - dot_nn(m0, basis0[...]) - dot_nn(m1, basis1[...])
    outs[3].start()
    for copy in outs:
        copy.wait()


def trailing_kernel(
    place, cols_in, from0, from1, from2, from3, row_in, feat_in, extra_in, left_in, m_in, basis_m_in,
    out,
    cols, pieces, row_feat, feat, extra, left, m, basis_m, near, result, sems, col_sems, out_sems,
):
    quarters = (from0, from1, from2, from3)
    small = fetch(
        [(a.at[:, pl.ds(56, 8), :], pieces.at[k]) for k, a in enumerate(quarters)]
        + [(feat_in, feat), (row_in, row_feat)],
        sems,
    )
    lanes = pl.ds(pl.multiple_of(place[1] % 4 * TILE, TILE), TILE)
    own_left = left_in.at[place[1] // 4, :, lanes]
    pairs = [(m_in, m), (basis_m_in, basis_m), (cols_in.at[0], cols.at[0]), (extra_in, extra)]
    pairs += [(cols_in.at[x], cols.at[x]) for x in range(1, NX)] + [(own_left, left)]
    copies = fetch(pairs, col_sems)
    for copy in small:
        copy.wait()
    slot = slots(place)
    col_feat = [
        site_tile([pieces[slot[tile % 4], 4 * (tile // 4) + j] for j in range(4)])
        for tile in range(8)
    ]
    for x in range(NX):
        for h in range(0 if x else 1, 2):
            near[x, h * TILE : (h + 1) * TILE, :] = near_dot(col_feat[h * 4 + x], feat[8:, :])
    near[0, :TILE, :] = jnp.zeros((TILE, FIRST), jnp.float32)
    row = lax.broadcasted_iota(jnp.int32, (256, TILE), 0)
    lane = lax.broadcasted_iota(jnp.int32, (256, TILE), 1)
    zero = (row < TILE) & (place[0] < 8)
    row_global = global_rows(place, TILE)
    for tile in range(1, 8):
        same = row_global == (tile * 8 + place[1]) * TILE + lane
        own = near_dot(row_feat[8:, :], col_feat[tile]) + jnp.where(same, nugget, 0.0)
        result[:, tile * TILE : (tile + 1) * TILE] = own
    outs = []
    for x in range(NX):
        for copy in copies[:4] if x == 0 else copies[3 + x : 4 + x]:
            copy.wait()
        cross = jnp.concatenate([cols[x, c, :256, :] for c in range(NC)], axis=1) + near[x]
        basis_c = jnp.concatenate(
            [
                jnp.concatenate(
                    [cols[x, c, 256 + l * 32 : 288 + l * 32, :] for l in range(4)], axis=1
                )
                for c in range(NC)
            ],
            axis=0,
        )
        value = dot_nt(basis_m[...], basis_c) - dot_nt(m[...], cross)
        for h in range(2):
            tile = h * 4 + x
            if tile == 0:
                copies[7].wait()
                result[:, :TILE] = left[...]
            else:
                span = slice(tile * TILE, (tile + 1) * TILE)
                own = value[:, h * TILE : (h + 1) * TILE] + result[:, span] + extra[:, span]
                result[:, span] = jnp.where(zero, 0.0, own)
            span = pl.ds(tile * TILE, TILE)
            outs.append(
                pltpu.make_async_copy(result.at[:, span], out.at[:, span], out_sems.at[tile])
            )
            outs[-1].start()
    for copy in outs:
        copy.wait()


SMEM = pl.BlockSpec(memory_space=pltpu.SMEM)
HBM = pl.BlockSpec(memory_space=pltpu.HBM)


def call(kernel, place, inputs, outs, scratch, sems, us):
    return pl.pallas_call(
        kernel,
        out_shape=[jax.ShapeDtypeStruct(shape, jnp.float32) for shape in outs],
        in_specs=[SMEM] + [HBM] * len(inputs),
        out_specs=[HBM] * len(outs),
        scratch_shapes=[pltpu.VMEM(shape, jnp.float32) for shape in scratch]
        + [pltpu.SemaphoreType.DMA((n,)) for n in sems],
        compiler_params=pltpu.CompilerParams(vmem_limit_bytes=58 * 2**20),
        cost_estimate=pl.CostEstimate(
            flops=us * 10**9, bytes_accessed=us * 3 * 10**6, transcendentals=0
        ),
    )(place, *inputs)


SQUARE, ROWS, FEAT = (PANEL, PANEL), (256, PANEL), (16, FIRST)
WORK, STRIPS = (PANEL, 2 * PANEL), (NC, 272, TILE)


def panel0(place, *inputs):
    outs = [SQUARE, SQUARE, ROWS, FEAT, (16, 256)]
    scratch = [(2, 4, 4, 4, 40, TILE), STRIPS, ROWS, SQUARE, ROWS, FEAT, (16, 256), WORK]
    return call(panel0_kernel, place, inputs, outs, scratch, (10, 5), 25)


def panel1(place, *inputs):
    outs = [(2, 256, PANEL), (256, FIRST), ROWS]
    scratch = [
        (2, 4, 4, 4, 48, TILE), (4, 256, TILE), SQUARE, SQUARE, ROWS, ROWS, FEAT, (16, 256), WORK,
        SQUARE, SQUARE, ROWS, (256, FIRST), ROWS,
    ]
    return call(panel1_kernel, place, inputs, outs, scratch, (15, 4), 35)


def trailing(place, *inputs):
    scratch = [
        (NX, NZ, 384, TILE), (NX, NZ, 8, TILE), (16, 256), FEAT, (256, FIRST), (256, TILE),
        (256, FIRST), ROWS, (NX, 256, FIRST), (256, FIRST),
    ]
    return call(trailing_kernel, place, inputs, [(256, FIRST)], scratch, (6, 8, 8), 10)[0]


def spread_to(value, axis, count, groups=None):
    every = jnp.broadcast_to(value[None], (count,) + value.shape)
    return lax.all_to_all(every, axis, 0, 0, axis_index_groups=groups)


def after(value, done):
    return jnp.where(done == done, value, jnp.zeros_like(value))


def lane_groups(rows):
    n = rows.shape[0]
    return rows.reshape(n, 4, TILE).transpose(1, 0, 2).reshape(4 * n, TILE)


def local(site_coords, basis_rows, extra_cov):
    my_row = lax.axis_index("row")
    my_col = lax.axis_index("col")
    place = jnp.stack([my_row, my_col]).astype(jnp.int32)
    z_groups = [[x * NZ + z for z in range(NZ)] for x in range(NX)]
    places = [(x, z, c) for x in range(NX) for z in range(NZ) for c in range(NC)]
    strip = extra_cov[:, :TILE]

    sites = site_coords.astype(jnp.float32)
    square = jnp.sum(sites * sites, axis=0, keepdims=True)
    one, none = jnp.ones((1, 32), jnp.float32), jnp.zeros((3, 32), jnp.float32)
    own_feat = jnp.concatenate([sites, square, one, none, -2.0 * sites, one, square, none])
    own_feat = jnp.pad(own_feat, ((0, 0), (0, 96)))

    def piece_of(r, c):
        return 4 * r + c % 4 + 128 * (c // 4)

    to_rows = [(piece_of(x * NZ + z, c), (x * NZ + z) * NC + c) for x, z, c in places]
    to_cols = [(piece_of(x * NZ + c, z), (x * NZ + z) * NC + c) for x, z, c in places]
    col_piece = lax.ppermute(own_feat[:8], BOTH, to_cols)
    row_piece = lax.ppermute(own_feat, BOTH, to_rows)

    half = my_col // 4
    extra_part = strip[:TILE].reshape(2, 4, 16, TILE).transpose(1, 0, 2, 3)
    basis_part = basis_rows[:TILE].reshape(2, 4, 2, 8, 4, TILE)
    basis_part = lax.dynamic_slice(
        basis_part, (0, my_col % 4, half, 0, 0, 0), (2, 1, 1, 8, 4, TILE)
    )
    basis_part = basis_part.reshape(2, 8, 4, TILE).transpose(2, 0, 1, 3)
    feat_part = jnp.broadcast_to(own_feat.reshape(1, 2, 1, 8, TILE), (2, 2, 2, 8, TILE))
    parts = jnp.concatenate(
        [extra_part, basis_part, feat_part.reshape(4, 2, 8, TILE)], axis=2
    ).reshape(8, 32, TILE)
    x_groups = [
        [(x * NZ + z) * NC + q + 4 * h for x in range(NX) for h in range(2)]
        for z in range(NZ)
        for q in range(4)
    ]
    over_x = lax.all_to_all(parts, BOTH, 0, 0, axis_index_groups=x_groups)
    first_of = jnp.where(half == 0, over_x[0, 24:], over_x[1, 24:])
    pack = jnp.concatenate(
        [over_x[0, :16], over_x[0, 16:24], over_x[1, 16:24], first_of, over_x[1, :16], col_piece]
    )
    over_z = spread_to(pack, "row", NZ, z_groups)

    turn = [((x * NZ + z) * NC + c, (x * NZ + c) * NC + z) for x, z, c in places]
    for_cols = lane_groups(lax.dynamic_slice_in_dim(basis_rows, my_col * 32, 32, 0))
    for_cols = after(jnp.concatenate([strip, for_cols]), over_z[0, 0, 0])
    turned = lax.ppermute(for_cols, BOTH, turn)

    quarters = [over_z] + [
        lax.ppermute(
            over_z, "row", [(x * NZ + z, (x + k) % NX * NZ + z) for x in range(NX) for z in range(NZ)]
        )
        for k in range(1, NX)
    ]
    def along_y(value):
        return [value] + [
            lax.ppermute(value, "col", [(c, (c + 2 * k) % NC) for c in range(NC)])
            for k in range(1, 4)
        ]

    def from_other_core(values):
        return [lax.ppermute(value, "col", [(c, c ^ 1) for c in range(NC)]) for value in values]

    owns = along_y(jnp.stack([quarter[:4, :40] for quarter in quarters]))
    others = from_other_core(owns)
    rest = [jnp.concatenate([quarter[4:, :32], quarter[4:, 40:56]], axis=1) for quarter in quarters]
    rest_owns = along_y(jnp.stack(rest))
    strips = lax.all_gather(jnp.concatenate([strip, row_piece]), "col", axis=0)
    turned = after(turned, quarters[3][0, 0, 0])
    cols_all = lax.all_gather(turned, "row", axis=0).reshape(NX, NZ, 384, TILE)

    v0, basis0, left0, feat, row_feat = panel0(place, *owns, *others, strips, basis_rows)
    rest_owns = [
        lax.dynamic_update_slice(own, after(own[:1, :1, :8], feat[0, 0]), (0, 0, 0, 0))
        for own in rest_owns
    ]
    rest_others = from_other_core(rest_owns)
    left, m, basis_m = panel1(
        place, *rest_owns, *rest_others, strips, v0, basis0, basis_rows, left0, feat, row_feat
    )
    return trailing(
        place, cols_all, *quarters, row_feat, feat, extra_cov, left, m, basis_m
    )


def solution(mesh):
    in_specs = (P(None, BOTH), P("row", None), P("row", "col"))
    out_specs = P("row", "col")
    return jax.shard_map(local, mesh=mesh, in_specs=in_specs, out_specs=out_specs, check_vma=False)
```

```python
import jax
import jax.numpy as jnp
from jax import lax
from jax.experimental import pallas as pl
from jax.experimental.pallas import tpu as pltpu
from jax.sharding import PartitionSpec as P

TILE = 128
PANEL = 512
FIRST = 1024
BLOCK = 16
NX, NZ, NC = 4, 8, 8

nugget = 0.5
range_cells = 3.0
highest = lax.Precision.HIGHEST
BOTH = ("row", "col")


def dot_nn(a, b):
    return lax.dot_general(
        a, b, (((1,), (0,)), ((), ())), precision=highest, preferred_element_type=jnp.float32
    )


def dot_nt(a, b):
    return lax.dot_general(
        a, b, (((1,), (1,)), ((), ())), precision=highest, preferred_element_type=jnp.float32
    )


def dot_tn(a, b):
    return lax.dot_general(
        a, b, (((0,), (0,)), ((), ())), precision=highest, preferred_element_type=jnp.float32
    )


def times_lower_t(a, v):
    half = v.shape[0] // 2
    return jnp.concatenate([dot_nt(a[:, :half], v[:half, :half]), dot_nt(a, v[half:, :])], axis=1)


def times_lower(a, v):
    half = v.shape[0] // 2
    return jnp.concatenate([dot_nn(a, v[:, :half]), dot_nn(a[:, half:], v[half:, half:])], axis=1)


def near_dot(a, b):
    return jnp.exp(jnp.sqrt(jnp.maximum(dot_tn(a, b), 0.0)) * (-1.0 / range_cells))


def reciprocal(x):
    r = pl.reciprocal(x, approx=True)
    return r * (2.0 - x * r)


def bf16_parts(v):
    high = v.astype(jnp.bfloat16)
    rest = v - high.astype(jnp.float32)
    mid = rest.astype(jnp.bfloat16)
    return high, mid, (rest - mid.astype(jnp.float32)).astype(jnp.bfloat16)


def stacked_dot(a, b, a_dim):
    a1, a2, a3 = bf16_parts(a)
    b1, b2, b3 = bf16_parts(b)
    left = jnp.concatenate([a3, a1, a2, a2, a1, a1], axis=a_dim)
    right = jnp.concatenate([b1, b3, b2, b1, b2, b1], axis=0)
    return lax.dot_general(
        left, right, (((a_dim,), (0,)), ((), ())), preferred_element_type=jnp.float32
    )


def eliminate(p, x, k):
    groups = p.shape[0] // 8
    sub = lax.broadcasted_iota(jnp.int32, (8, TILE), 0)

    def row(v, q):
        return jnp.broadcast_to(v[q // 8][q % 8 : q % 8 + 1], (8, TILE))

    p = [p[8 * g : 8 * g + 8] for g in range(groups)]
    x = [x[8 * g : 8 * g + 8] for g in range(groups)]
    cols = [
        [jnp.broadcast_to(p[g][:, k + q : k + q + 1], (8, TILE)) for g in range(groups)]
        for q in range(BLOCK)
    ]
    pivots = [jnp.zeros((8, TILE), jnp.float32) for _ in range(BLOCK // 8)]
    for q in range(0, BLOCK, 2):
        first, second = cols[q], cols[q + 1]
        a, b, d = row(first, q), row(second, q), row(second, q + 1)
        det = a * d - b * b
        r1, r2 = reciprocal(a), reciprocal(det)
        top, lo = q // 8, q % 8
        pivots[top] = jnp.where(sub == lo, a, jnp.where(sub == lo + 1, det * r1, pivots[top]))
        m1, m2 = [None] * groups, [None] * groups
        for g in range(top, groups):
            m1[g] = (d * first[g] - b * second[g]) * r2
            m2[g] = (a * second[g] - b * first[g]) * r2
            if g == top:
                m1[g] = jnp.where(sub > lo + 1, m1[g], jnp.where(sub == lo + 1, b * r1, 0.0))
                m2[g] = jnp.where(sub > lo + 1, m2[g], 0.0)
        for s in range(q + 2, BLOCK):
            u, v = row(cols[s], q), row(cols[s], q + 1)
            for g in range((q + 2) // 8, groups):
                cols[s][g] = cols[s][g] - m1[g] * u - m2[g] * v
        for w in (p, x):
            u, v = row(w, q), row(w, q + 1)
            for g in range(top, groups):
                w[g] = w[g] - m1[g] * u - m2[g] * v
    return jnp.concatenate(p, 0), jnp.concatenate(x, 0), jnp.concatenate(pivots, 0)


def factor_tile(t):
    row = lax.broadcasted_iota(jnp.int32, (TILE, TILE), 0)
    lane = lax.broadcasted_iota(jnp.int32, (TILE, TILE), 1)
    eye = jnp.where(row == lane, 1.0, 0.0).astype(jnp.float32)
    blocks = TILE // BLOCK
    ts = [t[b * BLOCK : (b + 1) * BLOCK] for b in range(blocks)]
    ws = [eye[b * BLOCK : (b + 1) * BLOCK] for b in range(blocks)]
    uppers, inverses = [], []
    for b in range(blocks):
        last = b + 1 == blocks
        both = slice(b, b + 1) if last else slice(b, b + 2)
        p, x, pivots = eliminate(
            jnp.concatenate(ts[both], 0), jnp.concatenate(ws[both], 0), b * BLOCK
        )
        scale = lax.rsqrt(pivots)
        uppers.append(p[:BLOCK] * scale)
        inverses.append(x[:BLOCK] * scale)
        if not last:
            ts[b + 1], ws[b + 1] = p[BLOCK:], x[BLOCK:]
        if b + 2 < blocks:
            prod = stacked_dot(
                uppers[b], jnp.concatenate([uppers[b], inverses[b]], axis=1), 0
            )
            for c in range(b + 2, blocks):
                rows = slice(c * BLOCK, (c + 1) * BLOCK)
                ts[c] = ts[c] - prod[rows, :TILE]
                ws[c] = ws[c] - prod[rows, TILE:]
    u = jnp.where(lane >= row, jnp.concatenate(uppers, 0), 0.0)
    return u, jnp.concatenate(inverses, 0)


def factor_in_place(work, tiles):
    n = tiles * TILE
    for j in range(tiles):
        rows = slice(j * TILE, (j + 1) * TILE)
        u, v = factor_tile(work[rows, rows])
        live = slice((j + 1) * TILE, n + j * TILE)
        work[rows, live] = stacked_dot(v, work[rows, live], 1)
        work[rows, rows] = u
        work[rows, n + j * TILE : n + (j + 1) * TILE] = v
        below = slice((j + 1) * TILE, n)
        if j + 1 < tiles:
            wide = slice((j + 1) * TILE, n + (j + 1) * TILE)
            work[below, wide] = work[below, wide] - stacked_dot(
                work[rows, below], work[rows, wide], 0
            )


def add_nugget(work):
    row = lax.broadcasted_iota(jnp.int32, (TILE, TILE), 0)
    lane = lax.broadcasted_iota(jnp.int32, (TILE, TILE), 1)
    diagonal = jnp.where(row == lane, nugget, 0.0).astype(jnp.float32)
    for z in range(4):
        rows = slice(z * TILE, (z + 1) * TILE)
        work[rows, rows] = work[rows, rows] + diagonal


def global_rows(place, width):
    row = lax.broadcasted_iota(jnp.int32, (256, width), 0)
    return jnp.where(row < TILE, row + place[0] * TILE, row + (place[0] + 31) * TILE)


def keep_lower(value, place, start):
    lane = lax.broadcasted_iota(jnp.int32, (256, PANEL), 1)
    return jnp.where(global_rows(place, PANEL) - start >= lane, value, 0.0)


def place_basis(part, offset, basis):
    for c in range(NC):
        for z in range(4):
            for l in range(4):
                basis[z * TILE + c * 16 : z * TILE + c * 16 + 16, l * TILE : (l + 1) * TILE] = (
                    part(c, z)[offset + l * 16 : offset + l * 16 + 16, :]
                )


def extra_rows(part, offset, first):
    halves = []
    for z in range(first, first + 2):
        for h in range(2):
            halves.append(
                jnp.concatenate(
                    [part(h * 4 + q, z)[offset : offset + 64, :] for q in range(4)], axis=1
                )
            )
    return jnp.concatenate(halves, axis=0)


def site_tile(pieces):
    value = pieces[0]
    for j in range(1, 4):
        value = value + pltpu.roll(pieces[j], 32 * j, 1)
    return value


def fetch(pairs, sems):
    copies = [pltpu.make_async_copy(a, b, sems.at[i]) for i, (a, b) in enumerate(pairs)]
    for copy in copies:
        copy.start()
    return copies


def near_rows(place, row_feat, right_feat, start):
    near = near_dot(row_feat[:8, :], right_feat[8:, start : start + PANEL])
    lane = lax.broadcasted_iota(jnp.int32, (256, PANEL), 1)
    return near + jnp.where(global_rows(place, PANEL) - start == lane, nugget, 0.0)


def from_cols(place, parts, owns, others):
    core, y = place[1] % 2, place[1] // 2
    return [
        (piece, parts.at[k, (y + 4 - shift) % 4])
        for k, pieces in ((core, owns), (1 - core, others))
        for shift, piece in enumerate(pieces)
    ]


def panel0_kernel(
    place, own0, own1, own2, own3, other0, other1, other2, other3, strips, basis_rows,
    v_out, basis_out, left_out, feat_out, row_out,
    parts, strip, phi, basis, left0, feat, row_feat, work, sems, out_sems,
):
    pairs = from_cols(place, parts, (own0, own1, own2, own3), (other0, other1, other2, other3))
    copies = fetch(pairs + [(strips, strip), (basis_rows, phi)], sems)
    work[:, PANEL:] = jnp.zeros((PANEL, PANEL), jnp.float32)
    for copy in copies[:8]:
        copy.wait()

    def part(c, z):
        return parts.at[c % 2, c // 2, z]

    place_basis(part, 64, basis)
    for z in range(4):
        for h in range(2):
            lanes = slice((2 * z + h) * TILE, (2 * z + h + 1) * TILE)
            feat[:, lanes] = site_tile([part(4 * h + j, z)[128:144, :] for j in range(4)])
    outs = [
        pltpu.make_async_copy(basis, basis_out, out_sems.at[0]),
        pltpu.make_async_copy(feat, feat_out, out_sems.at[1]),
        pltpu.make_async_copy(work.at[:, pl.ds(PANEL, PANEL)], v_out, out_sems.at[2]),
        pltpu.make_async_copy(left0, left_out, out_sems.at[3]),
        pltpu.make_async_copy(row_feat, row_out, out_sems.at[4]),
    ]
    outs[0].start()
    outs[1].start()
    for z in range(0, 4, 2):
        rows = slice(z * TILE, (z + 2) * TILE)
        near = near_dot(feat[:8, rows], feat[8:, :PANEL])
        work[rows, :PANEL] = extra_rows(part, 0, z) + near + dot_nt(basis[rows, :], basis[...])
    add_nugget(work)
    factor_in_place(work, 4)
    outs[2].start()
    for copy in copies[8:]:
        copy.wait()
    for h in range(2):
        pieces = [strip[4 * h + j, 256:272, :] for j in range(4)]
        row_feat[:, h * TILE : (h + 1) * TILE] = site_tile(pieces)
    outs[4].start()
    extra = jnp.concatenate([strip[q, :256, :] for q in range(4)], axis=1)
    a = extra + near_rows(place, row_feat, feat, 0) + dot_nt(phi[...], basis[...])
    left0[...] = keep_lower(times_lower_t(a, work[:, PANEL:]), place, 0)
    outs[3].start()
    for copy in outs:
        copy.wait()


def panel1_kernel(
    place, own0, own1, own2, own3, other0, other1, other2, other3, strips, v0_in, basis0_in,
    basis_rows, left0_in, feat_in, row_in,
    left_out, m_out, basis_m_out,
    parts, strip, v0, basis0, phi, left0, feat, row_feat, work, basis1, l10, left1, m, basis_m,
    sems, out_sems,
):
    pairs = from_cols(place, parts, (own0, own1, own2, own3), (other0, other1, other2, other3))
    copies = fetch(
        pairs
        + [
            (feat_in, feat),
            (basis0_in, basis0),
            (v0_in, v0),
            (strips.at[pl.ds(4, 4), pl.ds(0, 256), :], strip),
            (basis_rows, phi),
            (left0_in, left0),
            (row_in, row_feat),
        ],
        sems,
    )
    work[:, PANEL:] = jnp.zeros((PANEL, PANEL), jnp.float32)
    for copy in copies[:9]:
        copy.wait()

    def part(c, z):
        return parts.at[c % 2, c // 2, z]

    place_basis(part, 64, basis1)
    for z in range(0, 4, 2):
        rows = slice(z * TILE, (z + 2) * TILE)
        near = near_dot(feat[:8, PANEL + z * TILE : PANEL + (z + 2) * TILE], feat[8:, :])
        l10[rows, :] = extra_rows(part, 0, z) + near[:, :PANEL]
        work[rows, :PANEL] = extra_rows(part, 128, z) + near[:, PANEL:]
    for copy in copies[9:]:
        copy.wait()
    for z in range(0, 4, 2):
        rows = slice(z * TILE, (z + 2) * TILE)
        a10 = l10[rows, :] + dot_nt(basis1[rows, :], basis0[...])
        l10[rows, :] = times_lower_t(a10, v0[...])
    for z in range(0, 4, 2):
        rows = slice(z * TILE, (z + 2) * TILE)
        cols = slice(z * TILE, PANEL)
        work[rows, cols] = (
            work[rows, cols]
            + dot_nt(basis1[rows, :], basis1[cols, :])
            - dot_nt(l10[rows, :], l10[cols, :])
        )
    add_nugget(work)
    extra = jnp.concatenate([strip[q] for q in range(4)], axis=1)
    left1[...] = (
        extra
        + near_rows(place, row_feat, feat, PANEL)
        + dot_nt(phi[...], basis1[...])
        - dot_nt(left0[...], l10[...])
    )
    factor_in_place(work, 4)
    v1 = work[:, PANEL:]
    left1[...] = keep_lower(times_lower_t(left1[...], v1), place, PANEL)
    outs = [
        pltpu.make_async_copy(left0, left_out.at[0], out_sems.at[0]),
        pltpu.make_async_copy(left1, left_out.at[1], out_sems.at[1]),
        pltpu.make_async_copy(m, m_out, out_sems.at[2]),
        pltpu.make_async_copy(basis_m, basis_m_out, out_sems.at[3]),
    ]
    outs[0].start()
    outs[1].start()
    m1 = times_lower(left1[...], v1)
    m0 = times_lower(left0[...] - dot_nn(m1, l10[...]), v0[...])
    m[:, :PANEL] = m0
    m[:, PANEL:] = m1
    outs[2].start()
    basis_m[...] = phi[...] - dot_nn(m0, basis0[...]) - dot_nn(m1, basis1[...])
    outs[3].start()
    for copy in outs:
        copy.wait()


def trailing_kernel(
    place, cols_in, row_in, feat_in, extra_in, left_in, m_in, basis_m_in,
    out,
    cols, pieces, row_feat, feat, extra, left, m, basis_m, near, result, sems, col_sems, out_sems,
):
    small = fetch(
        [
            (cols_in.at[:, :, pl.ds(384, 16), :], pieces),
            (feat_in, feat),
            (row_in, row_feat),
            (extra_in, extra),
        ],
        sems,
    )
    lanes = pl.ds(pl.multiple_of(place[1] % 4 * TILE, TILE), TILE)
    own_left = left_in.at[place[1] // 4, :, lanes]
    copies = fetch([(m_in, m), (basis_m_in, basis_m), (own_left, left)], sems.at[pl.ds(4, 3)])

    def col_copy(x):
        return pltpu.make_async_copy(
            cols_in.at[x, :, pl.ds(0, 384), :], cols.at[x], col_sems.at[x]
        )

    def out_copy(tile):
        span = pl.ds(pl.multiple_of(tile * TILE, TILE), TILE)
        return pltpu.make_async_copy(result.at[:, span], out.at[:, span], out_sems.at[tile])

    for x in range(NX):
        col_copy(x).start()
    for copy in small:
        copy.wait()
    row = lax.broadcasted_iota(jnp.int32, (256, TILE), 0)
    lane = lax.broadcasted_iota(jnp.int32, (256, TILE), 1)
    zero = (row < TILE) & (place[0] < 8)
    row_global = global_rows(place, TILE)

    def near_step(x, carry):
        col_feat = jnp.concatenate(
            [site_tile([pieces[x, 4 * h + j] for j in range(4)]) for h in range(2)], axis=1
        )
        near[x] = near_dot(col_feat[:8], feat[8:, :])
        own = near_dot(row_feat[:8, :], col_feat[8:])
        for h in range(2):
            tile = h * 4 + x
            span = pl.ds(pl.multiple_of(tile * TILE, TILE), TILE)
            same = row_global == (tile * 8 + place[1]) * TILE + lane
            part = own[:, h * TILE : (h + 1) * TILE] + extra[:, span]
            result[:, span] = part + jnp.where(same, nugget, 0.0)
        return carry

    lax.fori_loop(0, NX, near_step, 0)
    for copy in copies:
        copy.wait()

    def step(x, carry):
        col_copy(x).wait()
        cross = jnp.concatenate([cols[x, c, :256, :] for c in range(NC)], axis=1) + near[x]
        basis_c = jnp.concatenate(
            [
                jnp.concatenate(
                    [cols[x, c, 256 + l * 32 : 288 + l * 32, :] for l in range(4)], axis=1
                )
                for c in range(NC)
            ],
            axis=0,
        )
        value = dot_nt(basis_m[...], basis_c) - dot_nt(m[...], cross)
        for h in range(2):
            span = pl.ds(pl.multiple_of((h * 4 + x) * TILE, TILE), TILE)
            part = value[:, h * TILE : (h + 1) * TILE] + result[:, span]
            result[:, span] = jnp.where(zero, 0.0, part)

        @pl.when(x == 0)
        def _():
            result[:, :TILE] = left[...]

        out_copy(x).start()
        out_copy(x + 4).start()
        return carry

    lax.fori_loop(0, NX, step, 0)
    for tile in range(8):
        out_copy(tile).wait()


SMEM = pl.BlockSpec(memory_space=pltpu.SMEM)
HBM = pl.BlockSpec(memory_space=pltpu.HBM)


def call(kernel, place, inputs, outs, scratch, sems, us):
    return pl.pallas_call(
        kernel,
        out_shape=[jax.ShapeDtypeStruct(shape, jnp.float32) for shape in outs],
        in_specs=[SMEM] + [HBM] * len(inputs),
        out_specs=[HBM] * len(outs),
        scratch_shapes=[pltpu.VMEM(shape, jnp.float32) for shape in scratch]
        + [pltpu.SemaphoreType.DMA((n,)) for n in sems],
        compiler_params=pltpu.CompilerParams(vmem_limit_bytes=58 * 2**20),
        cost_estimate=pl.CostEstimate(
            flops=us * 10**9, bytes_accessed=us * 3 * 10**6, transcendentals=0
        ),
    )(place, *inputs)


SQUARE, ROWS, FEAT = (PANEL, PANEL), (256, PANEL), (16, FIRST)
WORK, STRIPS = (PANEL, 2 * PANEL), (NC, 272, TILE)


def panel0(place, *inputs):
    outs = [SQUARE, SQUARE, ROWS, FEAT, (16, 256)]
    scratch = [(2, 4, 4, 144, TILE), STRIPS, ROWS, SQUARE, ROWS, FEAT, (16, 256), WORK]
    return call(panel0_kernel, place, inputs, outs, scratch, (10, 5), 25)


def panel1(place, *inputs):
    outs = [(2, 256, PANEL), (256, FIRST), ROWS]
    scratch = [
        (2, 4, 4, 192, TILE), (4, 256, TILE), SQUARE, SQUARE, ROWS, ROWS, FEAT, (16, 256), WORK,
        SQUARE, SQUARE, ROWS, (256, FIRST), ROWS,
    ]
    return call(panel1_kernel, place, inputs, outs, scratch, (15, 4), 35)


def trailing(place, *inputs):
    scratch = [
        (NX, NZ, 384, TILE), (NX, NZ, 16, TILE), (16, 256), FEAT, (256, FIRST), (256, TILE),
        (256, FIRST), ROWS, (NX, 256, FIRST), (256, FIRST),
    ]
    return call(trailing_kernel, place, inputs, [(256, FIRST)], scratch, (7, 4, 8), 10)[0]


def spread_to(value, axis, count, groups=None):
    every = jnp.broadcast_to(value[None], (count,) + value.shape)
    return lax.all_to_all(every, axis, 0, 0, axis_index_groups=groups)


def after(value, done):
    return jnp.where(done == done, value, jnp.zeros_like(value))


def lane_groups(rows):
    n = rows.shape[0]
    return rows.reshape(n, 4, TILE).transpose(1, 0, 2).reshape(4 * n, TILE)


def local(site_coords, basis_rows, extra_cov):
    my_row = lax.axis_index("row")
    my_col = lax.axis_index("col")
    place = jnp.stack([my_row, my_col]).astype(jnp.int32)
    z_groups = [[x * NZ + z for z in range(NZ)] for x in range(NX)]
    places = [(x, z, c) for x in range(NX) for z in range(NZ) for c in range(NC)]
    strip = extra_cov[:, :TILE]

    sites = site_coords.astype(jnp.float32)
    square = jnp.sum(sites * sites, axis=0, keepdims=True)
    one, none = jnp.ones((1, 32), jnp.float32), jnp.zeros((3, 32), jnp.float32)
    own_feat = jnp.concatenate([sites, square, one, none, -2.0 * sites, one, square, none])
    own_feat = jnp.pad(own_feat, ((0, 0), (0, 96)))

    def piece_of(r, c):
        return 4 * r + c % 4 + 128 * (c // 4)

    to_rows = [(piece_of(x * NZ + z, c), (x * NZ + z) * NC + c) for x, z, c in places]
    to_cols = [(piece_of(x * NZ + c, z), (x * NZ + z) * NC + c) for x, z, c in places]
    col_piece = lax.ppermute(own_feat, BOTH, to_cols)
    row_piece = lax.ppermute(own_feat, BOTH, to_rows)

    turn = [((x * NZ + z) * NC + c, (x * NZ + c) * NC + z) for x, z, c in places]
    basis_part = lane_groups(lax.dynamic_slice_in_dim(basis_rows, my_col * 32, 32, 0))
    turned = lax.ppermute(jnp.concatenate([strip, basis_part]), BOTH, turn)

    half = my_col // 4
    packs = []
    for h in range(2):
        piece = (my_col % 4 + 4 * h) * 16
        basis_16 = lane_groups(lax.dynamic_slice_in_dim(basis_rows, piece, 16, 0))
        basis_8 = lax.dynamic_slice_in_dim(basis_16, half * 32, 32, 0)
        packs.append(jnp.concatenate([strip[h * 64 : h * 64 + 64], basis_8, own_feat]))
    x_groups = [
        [(x * NZ + z) * NC + q + 4 * h for x in range(NX) for h in range(2)]
        for z in range(NZ)
        for q in range(4)
    ]
    pair = jnp.concatenate(packs).reshape(1, 2, 112, TILE)
    pair = jnp.broadcast_to(pair, (NX, 2, 112, TILE)).reshape(2 * NX, 112, TILE)
    over_x = lax.all_to_all(pair, BOTH, 0, 0, axis_index_groups=x_groups)
    first_of = jnp.where(half == 0, over_x[0, 96:], over_x[1, 96:])
    pack = jnp.concatenate(
        [over_x[0, :64], over_x[0, 64:96], over_x[1, 64:96], first_of, over_x[1, :64]]
    )
    over_z = spread_to(after(pack, turned[0, 0]), "row", NZ, z_groups)

    def along_y(value):
        return [value] + [
            lax.ppermute(value, "col", [(c, (c + 2 * k) % NC) for c in range(NC)])
            for k in range(1, 4)
        ]

    def from_other_core(values):
        return [lax.ppermute(value, "col", [(c, c ^ 1) for c in range(NC)]) for value in values]

    owns = along_y(over_z[:4, :144])
    others = from_other_core(owns)
    rest_owns = along_y(jnp.concatenate([over_z[4:, :128], over_z[4:, 144:]], axis=1))
    strips = lax.all_gather(jnp.concatenate([strip, row_piece]), "col", axis=0)
    for_cols = after(jnp.concatenate([turned, col_piece]), over_z[0, 0, 0])
    cols_all = lax.all_gather(for_cols, "row", axis=0).reshape(NX, NZ, 400, TILE)

    v0, basis0, left0, feat, row_feat = panel0(place, *owns, *others, strips, basis_rows)
    rest_owns = [
        lax.dynamic_update_slice(own, after(own[:1, :8], feat[0, 0]), (0, 0, 0))
        for own in rest_owns
    ]
    rest_others = from_other_core(rest_owns)
    left, m, basis_m = panel1(
        place, *rest_owns, *rest_others, strips, v0, basis0, basis_rows, left0, feat, row_feat
    )
    return trailing(
        place, cols_all, row_feat, feat, extra_cov, left, m, basis_m
    )


def solution(mesh):
    in_specs = (P(None, BOTH), P("row", None), P("row", "col"))
    out_specs = P("row", "col")
    return jax.shard_map(local, mesh=mesh, in_specs=in_specs, out_specs=out_specs, check_vma=False)
```

```python
import jax
import jax.numpy as jnp
from jax import lax
from jax.experimental import pallas as pl
from jax.experimental.pallas import tpu as pltpu
from jax.sharding import PartitionSpec as P

TILE = 128
PANEL = 512
FIRST = 1024
BLOCK = 16
NX, NZ, NC = 4, 8, 8

nugget = 0.5
range_cells = 3.0
highest = lax.Precision.HIGHEST
BOTH = ("row", "col")


def dot_nn(a, b):
    return lax.dot_general(
        a, b, (((1,), (0,)), ((), ())), precision=highest, preferred_element_type=jnp.float32
    )


def dot_nt(a, b):
    return lax.dot_general(
        a, b, (((1,), (1,)), ((), ())), precision=highest, preferred_element_type=jnp.float32
    )


def dot_tn(a, b):
    return lax.dot_general(
        a, b, (((0,), (0,)), ((), ())), precision=highest, preferred_element_type=jnp.float32
    )


def times_lower_t(a, v):
    half = v.shape[0] // 2
    return jnp.concatenate([dot_nt(a[:, :half], v[:half, :half]), dot_nt(a, v[half:, :])], axis=1)


def times_lower(a, v):
    half = v.shape[0] // 2
    return jnp.concatenate([dot_nn(a, v[:, :half]), dot_nn(a[:, half:], v[half:, half:])], axis=1)


def near_dot(a, b):
    return jnp.exp(jnp.sqrt(jnp.maximum(dot_tn(a, b), 0.0)) * (-1.0 / range_cells))


def reciprocal(x):
    r = pl.reciprocal(x, approx=True)
    return r * (2.0 - x * r)


def bf16_parts(v):
    high = v.astype(jnp.bfloat16)
    rest = v - high.astype(jnp.float32)
    mid = rest.astype(jnp.bfloat16)
    return high, mid, (rest - mid.astype(jnp.float32)).astype(jnp.bfloat16)


def stacked_dot(a, b, a_dim):
    a1, a2, a3 = bf16_parts(a)
    b1, b2, b3 = bf16_parts(b)
    left = jnp.concatenate([a3, a1, a2, a2, a1, a1], axis=a_dim)
    right = jnp.concatenate([b1, b3, b2, b1, b2, b1], axis=0)
    return lax.dot_general(
        left, right, (((a_dim,), (0,)), ((), ())), preferred_element_type=jnp.float32
    )


def eliminate(p, x, k):
    groups = p.shape[0] // 8
    sub = lax.broadcasted_iota(jnp.int32, (8, TILE), 0)

    def row(v, q):
        return jnp.broadcast_to(v[q // 8][q % 8 : q % 8 + 1], (8, TILE))

    p = [p[8 * g : 8 * g + 8] for g in range(groups)]
    x = [x[8 * g : 8 * g + 8] for g in range(groups)]
    cols = [
        [jnp.broadcast_to(p[g][:, k + q : k + q + 1], (8, TILE)) for g in range(groups)]
        for q in range(BLOCK)
    ]
    pivots = [jnp.zeros((8, TILE), jnp.float32) for _ in range(BLOCK // 8)]
    for q in range(0, BLOCK, 2):
        first, second = cols[q], cols[q + 1]
        a, b, d = row(first, q), row(second, q), row(second, q + 1)
        det = a * d - b * b
        r1, r2 = reciprocal(a), reciprocal(det)
        top, lo = q // 8, q % 8
        pivots[top] = jnp.where(sub == lo, a, jnp.where(sub == lo + 1, det * r1, pivots[top]))
        m1, m2 = [None] * groups, [None] * groups
        for g in range(top, groups):
            m1[g] = (d * first[g] - b * second[g]) * r2
            m2[g] = (a * second[g] - b * first[g]) * r2
            if g == top:
                m1[g] = jnp.where(sub > lo + 1, m1[g], jnp.where(sub == lo + 1, b * r1, 0.0))
                m2[g] = jnp.where(sub > lo + 1, m2[g], 0.0)
        for s in range(q + 2, BLOCK):
            u, v = row(cols[s], q), row(cols[s], q + 1)
            for g in range((q + 2) // 8, groups):
                cols[s][g] = cols[s][g] - m1[g] * u - m2[g] * v
        for w in (p, x):
            u, v = row(w, q), row(w, q + 1)
            for g in range(top, groups):
                w[g] = w[g] - m1[g] * u - m2[g] * v
    return jnp.concatenate(p, 0), jnp.concatenate(x, 0), jnp.concatenate(pivots, 0)


def factor_tile(t):
    row = lax.broadcasted_iota(jnp.int32, (TILE, TILE), 0)
    lane = lax.broadcasted_iota(jnp.int32, (TILE, TILE), 1)
    eye = jnp.where(row == lane, 1.0, 0.0).astype(jnp.float32)
    blocks = TILE // BLOCK
    ts = [t[b * BLOCK : (b + 1) * BLOCK] for b in range(blocks)]
    ws = [eye[b * BLOCK : (b + 1) * BLOCK] for b in range(blocks)]
    uppers, inverses = [], []
    for b in range(blocks):
        last = b + 1 == blocks
        both = slice(b, b + 1) if last else slice(b, b + 2)
        p, x, pivots = eliminate(
            jnp.concatenate(ts[both], 0), jnp.concatenate(ws[both], 0), b * BLOCK
        )
        scale = lax.rsqrt(pivots)
        uppers.append(p[:BLOCK] * scale)
        inverses.append(x[:BLOCK] * scale)
        if not last:
            ts[b + 1], ws[b + 1] = p[BLOCK:], x[BLOCK:]
        if b + 2 < blocks:
            prod = stacked_dot(
                uppers[b], jnp.concatenate([uppers[b], inverses[b]], axis=1), 0
            )
            for c in range(b + 2, blocks):
                rows = slice(c * BLOCK, (c + 1) * BLOCK)
                ts[c] = ts[c] - prod[rows, :TILE]
                ws[c] = ws[c] - prod[rows, TILE:]
    u = jnp.where(lane >= row, jnp.concatenate(uppers, 0), 0.0)
    return u, jnp.concatenate(inverses, 0)


def factor_in_place(work, tiles):
    n = tiles * TILE
    for j in range(tiles):
        rows = slice(j * TILE, (j + 1) * TILE)
        u, v = factor_tile(work[rows, rows])
        live = slice((j + 1) * TILE, n + j * TILE)
        work[rows, live] = stacked_dot(v, work[rows, live], 1)
        work[rows, rows] = u
        work[rows, n + j * TILE : n + (j + 1) * TILE] = v
        below = slice((j + 1) * TILE, n)
        if j + 1 < tiles:
            wide = slice((j + 1) * TILE, n + (j + 1) * TILE)
            work[below, wide] = work[below, wide] - stacked_dot(
                work[rows, below], work[rows, wide], 0
            )


def add_nugget(work):
    row = lax.broadcasted_iota(jnp.int32, (TILE, TILE), 0)
    lane = lax.broadcasted_iota(jnp.int32, (TILE, TILE), 1)
    diagonal = jnp.where(row == lane, nugget, 0.0).astype(jnp.float32)
    for z in range(4):
        rows = slice(z * TILE, (z + 1) * TILE)
        work[rows, rows] = work[rows, rows] + diagonal


def global_rows(place, width):
    row = lax.broadcasted_iota(jnp.int32, (256, width), 0)
    return jnp.where(row < TILE, row + place[0] * TILE, row + (place[0] + 31) * TILE)


def keep_lower(value, place, start):
    lane = lax.broadcasted_iota(jnp.int32, (256, PANEL), 1)
    return jnp.where(global_rows(place, PANEL) - start >= lane, value, 0.0)


def place_basis(part, offset, basis):
    for c in range(NC):
        for z in range(4):
            for l in range(4):
                basis[z * TILE + c * 16 : z * TILE + c * 16 + 16, l * TILE : (l + 1) * TILE] = (
                    part(c, z)[offset + l * 16 : offset + l * 16 + 16, :]
                )


def extra_rows(part, offset, first):
    halves = []
    for z in range(first, first + 2):
        for h in range(2):
            halves.append(
                jnp.concatenate(
                    [part(h * 4 + q, z)[offset : offset + 64, :] for q in range(4)], axis=1
                )
            )
    return jnp.concatenate(halves, axis=0)


def site_tile(pieces):
    value = pieces[0]
    for j in range(1, 4):
        value = value + pltpu.roll(pieces[j], 32 * j, 1)
    return value


def fetch(pairs, sems):
    copies = [pltpu.make_async_copy(a, b, sems.at[i]) for i, (a, b) in enumerate(pairs)]
    for copy in copies:
        copy.start()
    return copies


def near_rows(place, row_feat, right_feat, start):
    near = near_dot(row_feat[:8, :], right_feat[8:, start : start + PANEL])
    lane = lax.broadcasted_iota(jnp.int32, (256, PANEL), 1)
    return near + jnp.where(global_rows(place, PANEL) - start == lane, nugget, 0.0)


def from_cols(place, parts, owns, others):
    core, y = place[1] % 2, place[1] // 2
    return [
        (piece, parts.at[k, (y + 4 - shift) % 4])
        for k, pieces in ((core, owns), (1 - core, others))
        for shift, piece in enumerate(pieces)
    ]


def panel0_kernel(
    place, own0, own1, own2, own3, other0, other1, other2, other3, strips, basis_rows,
    v_out, basis_out, left_out, feat_out, row_out,
    parts, strip, phi, basis, left0, feat, row_feat, work, sems, out_sems,
):
    pairs = from_cols(place, parts, (own0, own1, own2, own3), (other0, other1, other2, other3))
    copies = fetch(pairs + [(strips, strip), (basis_rows, phi)], sems)
    work[:, PANEL:] = jnp.zeros((PANEL, PANEL), jnp.float32)
    for copy in copies[:8]:
        copy.wait()

    def part(c, z):
        return parts.at[c % 2, c // 2, z]

    place_basis(part, 64, basis)
    for z in range(4):
        for h in range(2):
            lanes = slice((2 * z + h) * TILE, (2 * z + h + 1) * TILE)
            feat[:, lanes] = site_tile([part(4 * h + j, z)[128:144, :] for j in range(4)])
    outs = [
        pltpu.make_async_copy(basis, basis_out, out_sems.at[0]),
        pltpu.make_async_copy(feat, feat_out, out_sems.at[1]),
        pltpu.make_async_copy(work.at[:, pl.ds(PANEL, PANEL)], v_out, out_sems.at[2]),
        pltpu.make_async_copy(left0, left_out, out_sems.at[3]),
        pltpu.make_async_copy(row_feat, row_out, out_sems.at[4]),
    ]
    outs[0].start()
    outs[1].start()
    for z in range(0, 4, 2):
        rows = slice(z * TILE, (z + 2) * TILE)
        near = near_dot(feat[:8, rows], feat[8:, :PANEL])
        work[rows, :PANEL] = extra_rows(part, 0, z) + near + dot_nt(basis[rows, :], basis[...])
    add_nugget(work)
    factor_in_place(work, 4)
    outs[2].start()
    for copy in copies[8:]:
        copy.wait()
    for h in range(2):
        pieces = [strip[4 * h + j, 256:272, :] for j in range(4)]
        row_feat[:, h * TILE : (h + 1) * TILE] = site_tile(pieces)
    outs[4].start()
    extra = jnp.concatenate([strip[q, :256, :] for q in range(4)], axis=1)
    a = extra + near_rows(place, row_feat, feat, 0) + dot_nt(phi[...], basis[...])
    left0[...] = keep_lower(times_lower_t(a, work[:, PANEL:]), place, 0)
    outs[3].start()
    for copy in outs:
        copy.wait()


def panel1_kernel(
    place, own0, own1, own2, own3, other0, other1, other2, other3, strips, v0_in, basis0_in,
    basis_rows, left0_in, feat_in, row_in,
    left_out, m_out, basis_m_out,
    parts, strip, v0, basis0, phi, left0, feat, row_feat, work, basis1, l10, left1, m, basis_m,
    sems, out_sems,
):
    pairs = from_cols(place, parts, (own0, own1, own2, own3), (other0, other1, other2, other3))
    copies = fetch(
        pairs
        + [
            (feat_in, feat),
            (basis0_in, basis0),
            (v0_in, v0),
            (strips.at[pl.ds(4, 4), pl.ds(0, 256), :], strip),
            (basis_rows, phi),
            (left0_in, left0),
            (row_in, row_feat),
        ],
        sems,
    )
    work[:, PANEL:] = jnp.zeros((PANEL, PANEL), jnp.float32)
    for copy in copies[:9]:
        copy.wait()

    def part(c, z):
        return parts.at[c % 2, c // 2, z]

    place_basis(part, 64, basis1)
    for z in range(0, 4, 2):
        rows = slice(z * TILE, (z + 2) * TILE)
        near = near_dot(feat[:8, PANEL + z * TILE : PANEL + (z + 2) * TILE], feat[8:, :])
        l10[rows, :] = extra_rows(part, 0, z) + near[:, :PANEL]
        work[rows, :PANEL] = extra_rows(part, 128, z) + near[:, PANEL:]
    for copy in copies[9:]:
        copy.wait()
    for z in range(0, 4, 2):
        rows = slice(z * TILE, (z + 2) * TILE)
        a10 = l10[rows, :] + dot_nt(basis1[rows, :], basis0[...])
        l10[rows, :] = times_lower_t(a10, v0[...])
    for z in range(0, 4, 2):
        rows = slice(z * TILE, (z + 2) * TILE)
        cols = slice(z * TILE, PANEL)
        work[rows, cols] = (
            work[rows, cols]
            + dot_nt(basis1[rows, :], basis1[cols, :])
            - dot_nt(l10[rows, :], l10[cols, :])
        )
    add_nugget(work)
    extra = jnp.concatenate([strip[q] for q in range(4)], axis=1)
    left1[...] = (
        extra
        + near_rows(place, row_feat, feat, PANEL)
        + dot_nt(phi[...], basis1[...])
        - dot_nt(left0[...], l10[...])
    )
    factor_in_place(work, 4)
    v1 = work[:, PANEL:]
    left1[...] = keep_lower(times_lower_t(left1[...], v1), place, PANEL)
    outs = [
        pltpu.make_async_copy(left0, left_out.at[0], out_sems.at[0]),
        pltpu.make_async_copy(left1, left_out.at[1], out_sems.at[1]),
        pltpu.make_async_copy(m, m_out, out_sems.at[2]),
        pltpu.make_async_copy(basis_m, basis_m_out, out_sems.at[3]),
    ]
    outs[0].start()
    outs[1].start()
    m1 = times_lower(left1[...], v1)
    m0 = times_lower(left0[...] - dot_nn(m1, l10[...]), v0[...])
    m[:, :PANEL] = m0
    m[:, PANEL:] = m1
    outs[2].start()
    basis_m[...] = phi[...] - dot_nn(m0, basis0[...]) - dot_nn(m1, basis1[...])
    outs[3].start()
    for copy in outs:
        copy.wait()


def trailing_kernel(
    place, cols_in, strips, extra_in, left_in, m_in, basis_m_in, feat_in,
    out,
    cols, strip, extra, left, m, basis_m, feat, row_feat, result, sems, col_sems, out_sems,
):
    copies = fetch(
        [
            (m_in, m),
            (basis_m_in, basis_m),
            (feat_in, feat),
            (strips.at[:, pl.ds(256, 16), :], strip),
            (extra_in, extra),
            (left_in, left),
        ],
        sems,
    )

    def col_copy(x):
        return pltpu.make_async_copy(cols_in.at[x], cols.at[x], col_sems.at[x])

    def out_copy(tile):
        lanes = pl.ds(pl.multiple_of(tile * TILE, TILE), TILE)
        return pltpu.make_async_copy(result.at[:, lanes], out.at[:, lanes], out_sems.at[tile])

    for x in range(NX):
        col_copy(x).start()
    for copy in copies:
        copy.wait()
    for h in range(2):
        row_feat[:, h * TILE : (h + 1) * TILE] = site_tile([strip[4 * h + j] for j in range(4)])
    row = lax.broadcasted_iota(jnp.int32, (256, TILE), 0)
    lane = lax.broadcasted_iota(jnp.int32, (256, TILE), 1)
    zero = (row < TILE) & (place[0] < 8)
    row_global = global_rows(place, TILE)

    def step(x, carry):
        col_copy(x).wait()
        col_feat = jnp.concatenate(
            [site_tile([cols[x, 4 * h + j, 384:400, :] for j in range(4)]) for h in range(2)],
            axis=1,
        )
        cross = jnp.concatenate([cols[x, c, :256, :] for c in range(NC)], axis=1)
        cross = cross + near_dot(col_feat[:8], feat[8:, :])
        basis_c = jnp.concatenate(
            [
                jnp.concatenate(
                    [cols[x, c, 256 + l * 32 : 288 + l * 32, :] for l in range(4)], axis=1
                )
                for c in range(NC)
            ],
            axis=0,
        )
        value = near_dot(row_feat[:8, :], col_feat[8:])
        value = value + dot_nt(basis_m[...], basis_c) - dot_nt(m[...], cross)
        for h in range(2):
            tile = h * 4 + x
            lanes = pl.ds(pl.multiple_of(tile * TILE, TILE), TILE)
            same = row_global == (tile * 8 + place[1]) * TILE + lane
            part = value[:, h * TILE : (h + 1) * TILE] + extra[:, lanes]
            result[:, lanes] = jnp.where(zero, 0.0, part + jnp.where(same, nugget, 0.0))

        @pl.when(x == 0)
        def _():
            own = pl.ds(pl.multiple_of(place[1] % 4 * TILE, TILE), TILE)
            result[:, :TILE] = left[place[1] // 4, :, own]

        out_copy(x).start()
        out_copy(x + 4).start()
        return carry

    lax.fori_loop(0, NX, step, 0)
    for tile in range(8):
        out_copy(tile).wait()


SMEM = pl.BlockSpec(memory_space=pltpu.SMEM)
HBM = pl.BlockSpec(memory_space=pltpu.HBM)


def call(kernel, place, inputs, outs, scratch, sems, us):
    return pl.pallas_call(
        kernel,
        out_shape=[jax.ShapeDtypeStruct(shape, jnp.float32) for shape in outs],
        in_specs=[SMEM] + [HBM] * len(inputs),
        out_specs=[HBM] * len(outs),
        scratch_shapes=[pltpu.VMEM(shape, jnp.float32) for shape in scratch]
        + [pltpu.SemaphoreType.DMA((n,)) for n in sems],
        compiler_params=pltpu.CompilerParams(vmem_limit_bytes=58 * 2**20),
        cost_estimate=pl.CostEstimate(
            flops=us * 10**9, bytes_accessed=us * 3 * 10**6, transcendentals=0
        ),
    )(place, *inputs)


SQUARE, ROWS, FEAT = (PANEL, PANEL), (256, PANEL), (16, FIRST)
WORK, STRIPS = (PANEL, 2 * PANEL), (NC, 272, TILE)


def panel0(place, *inputs):
    outs = [SQUARE, SQUARE, ROWS, FEAT, (16, 256)]
    scratch = [(2, 4, 4, 144, TILE), STRIPS, ROWS, SQUARE, ROWS, FEAT, (16, 256), WORK]
    return call(panel0_kernel, place, inputs, outs, scratch, (10, 5), 25)


def panel1(place, *inputs):
    outs = [(2, 256, PANEL), (256, FIRST), ROWS]
    scratch = [
        (2, 4, 4, 192, TILE), (4, 256, TILE), SQUARE, SQUARE, ROWS, ROWS, FEAT, (16, 256), WORK,
        SQUARE, SQUARE, ROWS, (256, FIRST), ROWS,
    ]
    return call(panel1_kernel, place, inputs, outs, scratch, (15, 4), 35)


def trailing(place, *inputs):
    scratch = [
        (NX, NZ, 400, TILE), (NC, 16, TILE), (256, FIRST), (2, 256, PANEL), (256, FIRST), ROWS,
        FEAT, (16, 256), (256, FIRST),
    ]
    return call(trailing_kernel, place, inputs, [(256, FIRST)], scratch, (6, 4, 8), 10)[0]


def spread_to(value, axis, count, groups=None):
    every = jnp.broadcast_to(value[None], (count,) + value.shape)
    return lax.all_to_all(every, axis, 0, 0, axis_index_groups=groups)


def after(value, done):
    return jnp.where(done == done, value, jnp.zeros_like(value))


def lane_groups(rows):
    n = rows.shape[0]
    return rows.reshape(n, 4, TILE).transpose(1, 0, 2).reshape(4 * n, TILE)


def local(site_coords, basis_rows, extra_cov):
    my_row = lax.axis_index("row")
    my_col = lax.axis_index("col")
    place = jnp.stack([my_row, my_col]).astype(jnp.int32)
    z_groups = [[x * NZ + z for z in range(NZ)] for x in range(NX)]
    places = [(x, z, c) for x in range(NX) for z in range(NZ) for c in range(NC)]
    strip = extra_cov[:, :TILE]

    sites = site_coords.astype(jnp.float32)
    square = jnp.sum(sites * sites, axis=0, keepdims=True)
    one, none = jnp.ones((1, 32), jnp.float32), jnp.zeros((3, 32), jnp.float32)
    own_feat = jnp.concatenate([sites, square, one, none, -2.0 * sites, one, square, none])
    own_feat = jnp.pad(own_feat, ((0, 0), (0, 96)))

    def piece_of(r, c):
        return 4 * r + c % 4 + 128 * (c // 4)

    to_rows = [(piece_of(x * NZ + z, c), (x * NZ + z) * NC + c) for x, z, c in places]
    to_cols = [(piece_of(x * NZ + c, z), (x * NZ + z) * NC + c) for x, z, c in places]
    col_piece = lax.ppermute(own_feat, BOTH, to_cols)
    row_piece = lax.ppermute(own_feat, BOTH, to_rows)

    turn = [((x * NZ + z) * NC + c, (x * NZ + c) * NC + z) for x, z, c in places]
    basis_part = lane_groups(lax.dynamic_slice_in_dim(basis_rows, my_col * 32, 32, 0))
    turned = lax.ppermute(jnp.concatenate([strip, basis_part]), BOTH, turn)

    half = my_col // 4
    packs = []
    for h in range(2):
        piece = (my_col % 4 + 4 * h) * 16
        basis_16 = lane_groups(lax.dynamic_slice_in_dim(basis_rows, piece, 16, 0))
        basis_8 = lax.dynamic_slice_in_dim(basis_16, half * 32, 32, 0)
        packs.append(jnp.concatenate([strip[h * 64 : h * 64 + 64], basis_8, own_feat]))
    x_groups = [
        [(x * NZ + z) * NC + q + 4 * h for x in range(NX) for h in range(2)]
        for z in range(NZ)
        for q in range(4)
    ]
    pair = jnp.concatenate(packs).reshape(1, 2, 112, TILE)
    pair = jnp.broadcast_to(pair, (NX, 2, 112, TILE)).reshape(2 * NX, 112, TILE)
    over_x = lax.all_to_all(pair, BOTH, 0, 0, axis_index_groups=x_groups)
    first_of = jnp.where(half == 0, over_x[0, 96:], over_x[1, 96:])
    pack = jnp.concatenate(
        [over_x[0, :64], over_x[0, 64:96], over_x[1, 64:96], first_of, over_x[1, :64]]
    )
    over_z = spread_to(after(pack, turned[0, 0]), "row", NZ, z_groups)

    def along_y(value):
        return [value] + [
            lax.ppermute(value, "col", [(c, (c + 2 * k) % NC) for c in range(NC)])
            for k in range(1, 4)
        ]

    def from_other_core(values):
        return [lax.ppermute(value, "col", [(c, c ^ 1) for c in range(NC)]) for value in values]

    owns = along_y(over_z[:4, :144])
    others = from_other_core(owns)
    rest_owns = along_y(jnp.concatenate([over_z[4:, :128], over_z[4:, 144:]], axis=1))
    strips = lax.all_gather(jnp.concatenate([strip, row_piece]), "col", axis=0)
    for_cols = after(jnp.concatenate([turned, col_piece]), over_z[0, 0, 0])
    cols_all = lax.all_gather(for_cols, "row", axis=0).reshape(NX, NZ, 400, TILE)

    v0, basis0, left0, feat, row_feat = panel0(place, *owns, *others, strips, basis_rows)
    rest_owns = [
        lax.dynamic_update_slice(own, after(own[:1, :8], feat[0, 0]), (0, 0, 0))
        for own in rest_owns
    ]
    rest_others = from_other_core(rest_owns)
    left, m, basis_m = panel1(
        place, *rest_owns, *rest_others, strips, v0, basis0, basis_rows, left0, feat, row_feat
    )
    return trailing(place, cols_all, strips, extra_cov, left, m, basis_m, feat)


def solution(mesh):
    in_specs = (P(None, BOTH), P("row", None), P("row", "col"))
    out_specs = P("row", "col")
    return jax.shard_map(local, mesh=mesh, in_specs=in_specs, out_specs=out_specs, check_vma=False)
```
